128 devices in a mesh: tensor: 4 (over y), dp: 32 (over z, x, core).
Axes of the slice: x: 4, y: 4, z: 4, core: 2. Of those that a mesh axis runs over, the one named last changes fastest.
Arguments:
- gradients: bfloat16 [32, 512, 128, 128], P('dp', 'tensor')
- residual: bfloat16 [32, 512, 128, 128], P('dp', 'tensor'), may hold values from -1.5 to 1.5
- momentum: bfloat16 [512, 128, 128], P('tensor'), may hold values from -6 to 6
- bitmap: int32 [32, 512], P('dp', 'tensor'), may hold values from 0 to 1, as said below
- starts: int32 [4, 32], replicated, may hold values from 0 to 127, as said below
Outputs:
- new_residual: bfloat16 [32, 512, 128, 128], P('dp', 'tensor')
- new_momentum: bfloat16 [512, 128, 128], P('tensor')
The draws below stay inside these ranges and needn't reach their ends.
Inputs may be any that keep to these rules, and one draw needn't show every extreme that they name: `bitmap`: in each tile shard one bucket of 7 tiles is selected by every replica; the other tiles are selected at random. `starts`: row k holds the first local tile of each of the 32 buckets of tile shard k, rising from 0; a bucket ends where the next begins, the last at 128; every bucket holds 1 to 7 tiles, and one in each row holds exactly 7.
All inputs are finite; a program needn't handle non-finite values.
Results may differ from the reference program's by a relative error of at most 0.015.
Values may be sent and summed in bfloat16 or wider, within the bound.
No kernel may reach another device: no remote copies, remote signals or barrier semaphores. Data moves between devices by JAX's collectives and lax.ppermute only.
A program may use at most 128 MiB of HBM per device.

```python
import math
import jax
import jax.numpy as jnp
from jax import lax

TILE = 128
TILES = 512
TILES_LOC = 128
MOST = 7
N_TENSOR = 4
N_DP = 32


def bucket_layout(key):
    mean_size = TILES_LOC // N_DP
    first_key, order_key = jax.random.split(jax.random.fold_in(key, 11))
    halves = jax.random.randint(first_key, (N_TENSOR, N_DP // 2), 1, 2 * mean_size)
    halves = halves.at[:, 0].set(2 * mean_size - 1)
    bucket_sizes = jnp.concatenate([halves, 2 * mean_size - halves], axis=1)
    order_keys = jax.random.split(order_key, N_TENSOR)
    orders = jax.vmap(lambda row_key: jax.random.permutation(row_key, N_DP))(order_keys)
    placed = jnp.take_along_axis(bucket_sizes, orders, axis=1)
    starts = (jnp.cumsum(placed, axis=1) - placed).astype(jnp.int32)
    full_bucket = jnp.argmin(orders, axis=1)
    full_start = jnp.take_along_axis(starts, full_bucket[:, None], axis=1)[:, 0]
    return (starts, full_start)


def draw_starts(key, part):
    starts, full_start = bucket_layout(key)
    return starts


def draw_bitmap(key, part):
    starts, full_start = bucket_layout(key)
    key = jax.random.fold_in(key, 5)
    coins = jax.random.randint(key, (N_DP, TILES), 0, 10) < 7
    positions = jnp.arange(TILES, dtype=jnp.int32)
    shard_of = positions // TILES_LOC
    local_pos = positions % TILES_LOC
    begin = full_start[shard_of]
    in_full = (local_pos >= begin) & (local_pos < begin + MOST)
    return jnp.where(coins | in_full[None, :], 1, 0).astype(jnp.int32)


def draw_gradients(key, part):
    key = jax.random.fold_in(key, 7)
    keys = jax.random.split(key, 4)
    tile_scale = jnp.exp(jax.random.uniform(keys[0], (1, TILES, 1, 1), jnp.float32, math.log(0.03), math.log(0.3)))
    row_scale = jnp.exp(jax.random.uniform(keys[1], (1, TILES, TILE, 1), jnp.float32, math.log(0.5), math.log(2.0)))
    col_scale = jnp.exp(jax.random.uniform(keys[2], (1, TILES, 1, TILE), jnp.float32, math.log(0.5), math.log(2.0)))
    rank_pos = jnp.arange(N_DP, dtype=jnp.float32).reshape(N_DP, 1, 1, 1) / (N_DP - 1)
    tile_pos = jnp.arange(TILES, dtype=jnp.float32).reshape(1, TILES, 1, 1) / (TILES - 1)
    noise = jax.random.normal(keys[3], (N_DP, TILES, TILE, TILE), jnp.float32) * (1.0 + 2.0 * rank_pos)
    values = noise * tile_scale * row_scale * col_scale * (1.0 + 2.0 * tile_pos)
    return values.astype(jnp.bfloat16)


def level_of(stream_key, shape, shards, least, largest):
    def one(position, blocks):
        draws = jax.random.uniform(jax.random.fold_in(jax.random.fold_in(stream_key, 6), position), (blocks,), jnp.float32, least / len(shards), largest / len(shards))
        return jnp.repeat(jnp.exp(draws), shape[position] // blocks).reshape((-1,) + (1,) * (len(shape) - position - 1))

    gain = one(*shards[0])
    for cut in shards[1:]:
        gain = gain * one(*cut)
    return gain


def normal_values(rng, dims, deviation, bound, cuts=(), kind=jnp.bfloat16):
    result = jax.random.normal(rng, dims, jnp.float32) * deviation
    if len(cuts) > 0:
        result = level_of(rng, dims, cuts, -0.22, 0.18) * result
    return jnp.clip(result, min=-bound, max=bound).astype(kind)


def setup_inputs(seed: int = 0) -> dict:
    splits = jax.random.split(jax.random.key(seed), 6)
    gradients = draw_gradients(jax.random.fold_in(splits[5], 71), 0)
    residual = normal_values(splits[1], (N_DP, TILES, TILE, TILE), 0.1, 1.5, ((0, 32), (1, 4)))
    momentum = normal_values(splits[2], (TILES, TILE, TILE), 1.5, 6.0, ((0, 4),))
    bitmap = draw_bitmap(jax.random.fold_in(splits[5], 71), 0)
    starts = draw_starts(jax.random.fold_in(splits[5], 71), 0)
    return {"gradients": gradients, "residual": residual, "momentum": momentum, "bitmap": bitmap, "starts": starts}


MOMENTUM = 0.9
CLIP_LEVEL = 3.0
EPSILON = 1e-06

def reference(gradients, residual, momentum, bitmap, starts):

    def one_replica(total_sum, inputs):
        grad_tiles, resid_tiles, chosen = inputs
        accumulated = grad_tiles.astype(jnp.float32) + resid_tiles.astype(jnp.float32)
        rounded = lax.optimization_barrier(accumulated.astype(jnp.bfloat16))
        selected = chosen[:, None, None] > 0
        zero_tiles = jnp.zeros_like(rounded)
        outgoing = jnp.where(selected, rounded, zero_tiles)
        left_over = jnp.where(selected, zero_tiles, rounded)
        return (total_sum + outgoing.astype(jnp.float32), left_over)
    initial = jnp.zeros(gradients.shape[1:], jnp.float32)
    summed, new_residual = lax.scan(one_replica, initial, (gradients, residual, bitmap))
    ends = jnp.concatenate([starts[:, 1:], jnp.full((N_TENSOR, 1), TILES_LOC, jnp.int32)], axis=1)
    bucket_sizes = ends - starts
    bucket_tiles = lax.optimization_barrier(jnp.sum(bucket_sizes, axis=0))
    local_tiles = jnp.arange(TILES_LOC, dtype=jnp.int32)
    owner_of = lax.optimization_barrier(jnp.sum((local_tiles[None, :, None] >= starts[:, None, :]).astype(jnp.int32), axis=2)) - 1
    owner_of = owner_of.reshape(TILES)
    membership = owner_of[:, None] == jnp.arange(N_DP, dtype=jnp.int32)[None, :]
    tile_squares = lax.optimization_barrier(jnp.sum(summed * summed, axis=(1, 2)))
    bucket_squares = lax.optimization_barrier(jnp.sum(jnp.where(membership, tile_squares[:, None], 0.0), axis=0))
    bucket_rms = jnp.sqrt(bucket_squares / (bucket_tiles.astype(jnp.float32) * float(TILE * TILE)) + EPSILON)
    clip_factor = jnp.minimum(1.0, CLIP_LEVEL / bucket_rms)
    tile_factor = lax.optimization_barrier(jnp.sum(jnp.where(membership, clip_factor[None, :], 0.0), axis=1))
    update_tiles = (summed * tile_factor[:, None, None]).astype(jnp.bfloat16)
    new_momentum = (MOMENTUM * momentum.astype(jnp.float32) + update_tiles.astype(jnp.float32)).astype(jnp.bfloat16)
    return (new_residual, new_momentum)
```

```python
import functools

import jax
import jax.numpy as jnp
from jax import lax
from jax.experimental import pallas as pl
from jax.experimental.pallas import tpu as pltpu
from jax.sharding import PartitionSpec as P

MOMENTUM = 0.9
CLIP_LEVEL = 3.0
EPSILON = 1e-06
STREAMS = 2
BLOCK = 8
SHIFTS = (1, 3, 2, 0)
BF16 = jnp.bfloat16
F32 = jnp.float32


def dp_index(z, x, core):
    return (z * 4 + x) * 2 + core


def each_dp():
    return [(d, d // 8, (d // 2) % 4, d % 2) for d in range(32)]


def swap_core():
    return [(d, d ^ 1) for d in range(32)]


def shift_first(k):
    pairs = []
    for d, z, x, core in each_dp():
        to = dp_index(z, (x + k) % 4, core) if core == 0 else dp_index((z + k) % 4, x, core)
        pairs.append((d, to))
    return pairs


def swap_second(mask):
    pairs = []
    for d, z, x, core in each_dp():
        to = dp_index(z ^ mask, x, core) if core == 0 else dp_index(z, x ^ mask, core)
        pairs.append((d, to))
    return pairs


def shift_tensor(k):
    return [(i, (i + k) % 4) for i in range(4)]


def tile_block(index_map):
    return pl.BlockSpec((BLOCK, 128, 128), index_map)


def blocks_shape(count):
    return jax.ShapeDtypeStruct((count * BLOCK, 128, 128), BF16)


def params():
    return pltpu.CompilerParams(vmem_limit_bytes=40 * 1024 * 1024)


def rounded_tile(g_ref, r_ref, t):
    return (g_ref[t].astype(F32) + r_ref[t].astype(F32)).astype(BF16)


def outgoing_kernel(index_ref, bitmap_ref, g_ref, r_ref, out_ref):
    first = index_ref[pl.program_id(0)] * BLOCK
    for t in range(BLOCK):
        value = rounded_tile(g_ref, r_ref, t)
        out_ref[t] = jnp.where(bitmap_ref[first + t] > 0, value, jnp.zeros_like(value))


def outgoing_blocks(index, bitmap, gradients, residual):
    count = index.shape[0]
    return pl.pallas_call(
        outgoing_kernel,
        grid_spec=pltpu.PrefetchScalarGridSpec(
            num_scalar_prefetch=2,
            grid=(count,),
            in_specs=[tile_block(lambda i, index, bitmap: (index[i], 0, 0))] * 2,
            out_specs=tile_block(lambda i, index, bitmap: (i, 0, 0)),
        ),
        out_shape=blocks_shape(count),
        compiler_params=params(),
        cost_estimate=pl.CostEstimate(
            flops=count * BLOCK * 16384, bytes_accessed=count * BLOCK * 98304, transcendentals=0
        ),
    )(index, bitmap, gradients, residual)


def residual_kernel(bitmap_ref, g_ref, r_ref, out_ref):
    tiles = out_ref.shape[0]
    first = pl.program_id(0) * tiles
    for t in range(tiles):
        value = rounded_tile(g_ref, r_ref, t)
        out_ref[t] = jnp.where(bitmap_ref[first + t] > 0, jnp.zeros_like(value), value)


def left_over(bitmap, gradients, residual):
    spec = pl.BlockSpec((16, 128, 128), lambda i, bitmap: (i, 0, 0))
    return pl.pallas_call(
        residual_kernel,
        grid_spec=pltpu.PrefetchScalarGridSpec(
            num_scalar_prefetch=1, grid=(8,), in_specs=[spec] * 2, out_specs=spec
        ),
        out_shape=blocks_shape(16),
        compiler_params=params(),
        cost_estimate=pl.CostEstimate(flops=2**21, bytes_accessed=3 * 2**22, transcendentals=0),
    )(bitmap, gradients, residual)


def pair_kernel(a_ref, b_ref, *out_refs):
    for k, out_ref in enumerate(out_refs):

        @pl.when(pl.program_id(0) == k)
        def _():
            out_ref[...] = (a_ref[...].astype(F32) + b_ref[...].astype(F32)).astype(BF16)


def pair_sums(a, b):
    count = a.shape[0] // BLOCK
    return pl.pallas_call(
        pair_kernel,
        grid=(count,),
        in_specs=[tile_block(lambda i: (i, 0, 0))] * 2,
        out_specs=[tile_block(lambda i: (0, 0, 0))] * count,
        out_shape=[blocks_shape(1)] * count,
        compiler_params=params(),
        cost_estimate=pl.CostEstimate(
            flops=count * BLOCK * 16384, bytes_accessed=count * BLOCK * 98304, transcendentals=0
        ),
    )(a, b)


def sum_kernel(*refs):
    out_ref = refs[-1]
    for t in range(BLOCK):
        total = refs[0][t].astype(F32)
        for ref in refs[1:-1]:
            total = total + ref[t].astype(F32)
        out_ref[t] = total.astype(BF16)


def block_sum(*blocks):
    spec = tile_block(lambda: (0, 0, 0))
    return pl.pallas_call(
        sum_kernel,
        in_specs=[spec] * len(blocks),
        out_specs=spec,
        out_shape=blocks_shape(1),
        compiler_params=params(),
        cost_estimate=pl.CostEstimate(
            flops=BLOCK * 65536, bytes_accessed=(1 + len(blocks)) * BLOCK * 32768, transcendentals=0
        ),
    )(*blocks)


def last_sum_kernel(first_ref, table_ref, a_ref, b_ref, out_ref, row_ref):
    lo, hi = table_ref[0:1, :], table_ref[1:2, :]
    row = jnp.zeros((1, 128), F32)
    for t in range(BLOCK):
        total = a_ref[t].astype(F32) + b_ref[t].astype(F32)
        out_ref[t] = total.astype(BF16)
        square = jnp.sum(jnp.sum(total * total, axis=0, keepdims=True), axis=1, keepdims=True)
        tile = first_ref[0] + t
        row = row + jnp.where((lo <= tile) & (tile < hi), square, 0.0)
    row_ref[...] = jnp.broadcast_to(row, (8, 128))


def last_sum(first, table, a, b):
    spec = tile_block(lambda i, first: (0, 0, 0))
    small = pl.BlockSpec((8, 128), lambda i, first: (0, 0))
    return pl.pallas_call(
        last_sum_kernel,
        grid_spec=pltpu.PrefetchScalarGridSpec(
            num_scalar_prefetch=1,
            grid=(1,),
            in_specs=[small, spec, spec],
            out_specs=[spec, small],
        ),
        out_shape=[blocks_shape(1), jax.ShapeDtypeStruct((8, 128), F32)],
        compiler_params=params(),
        cost_estimate=pl.CostEstimate(
            flops=BLOCK * 65536, bytes_accessed=3 * BLOCK * 32768, transcendentals=0
        ),
    )(first, table, a, b)


def final_kernel(index_ref, table_ref, mine_ref, other_ref, m_ref, *refs):
    block_refs, out_ref, factor_ref = refs[:-2], refs[-2], refs[-1]
    step = pl.program_id(0)

    @pl.when(step == 0)
    def _():
        lo, hi, count = table_ref[0:1, :], table_ref[1:2, :], table_ref[2:3, :]
        squares = mine_ref[0:1, :] + other_ref[0:1, :]
        rms = jnp.sqrt(squares / (count.astype(F32) * 16384.0) + EPSILON)
        clip = jnp.minimum(1.0, CLIP_LEVEL / rms)
        tile = lax.broadcasted_iota(jnp.int32, (128, 128), 0)
        chosen = jnp.where((lo <= tile) & (tile < hi), clip, 0.0)
        factor_ref[...] = jnp.broadcast_to(jnp.sum(chosen, axis=1, keepdims=True), (128, 128))

    first = index_ref[step] * BLOCK
    for k, block_ref in enumerate(block_refs):

        @pl.when(step == k)
        def _():
            for t in range(BLOCK):
                factor = factor_ref[pl.ds(first + t, 1), :]
                update = (block_ref[t].astype(F32) * factor).astype(BF16)
                out_ref[t] = (MOMENTUM * m_ref[t].astype(F32) + update.astype(F32)).astype(BF16)


def finish(index, table, mine, other, momentum, blocks):
    small = pl.BlockSpec((8, 128), lambda i, index: (0, 0))
    moved = tile_block(lambda i, index: (index[i], 0, 0))
    return pl.pallas_call(
        final_kernel,
        grid_spec=pltpu.PrefetchScalarGridSpec(
            num_scalar_prefetch=1,
            grid=(len(blocks),),
            in_specs=[small] * 3
            + [moved]
            + [tile_block(lambda i, index: (0, 0, 0))] * len(blocks),
            out_specs=moved,
            scratch_shapes=[pltpu.VMEM((128, 128), F32)],
        ),
        out_shape=blocks_shape(16),
        compiler_params=params(),
        cost_estimate=pl.CostEstimate(flops=2**23, bytes_accessed=3 * 2**22, transcendentals=0),
    )(index, table, mine, other, momentum, *blocks)


def row_sum(own, by_shift):
    r1, r2, r3 = by_shift
    return (own + r2) + (r1 + r3)


def shards(gradients, residual, momentum, bitmap, starts):
    gradients, residual, bitmap = gradients[0], residual[0], bitmap[0]
    dp = lax.axis_index("dp")
    z, x, core = dp // 8, (dp // 2) % 4, dp % 2
    mine = jnp.where(core == 0, x, z)
    theirs = jnp.where(core == 0, z, x)
    shifts = jnp.array(SHIFTS, jnp.int32)
    mine_to = core * 8 + ((mine + shifts) % 4) * 2
    theirs_to = (1 - core) * 8 + ((theirs + shifts) % 4) * 2
    mine_from = core * 8 + ((mine - shifts) % 4) * 2
    theirs_from = (1 - core) * 8 + ((theirs - shifts) % 4) * 2

    ends = jnp.concatenate([starts[:, 1:], jnp.full((4, 1), 128, jnp.int32)], axis=1)
    shard = lax.axis_index("tensor")
    lo = lax.dynamic_slice_in_dim(starts, shard, 1, 0)
    hi = lax.dynamic_slice_in_dim(ends, shard, 1, 0)
    count = jnp.sum(ends - starts, axis=0, keepdims=True)
    table = jnp.concatenate([lo, hi, count, jnp.zeros((5, 32), jnp.int32)], axis=0)
    table = jnp.pad(table, ((0, 0), (0, 96)), constant_values=128)

    sent = []
    for s in range(STREAMS):
        blocks = outgoing_blocks(theirs_to + s, bitmap, gradients, residual)
        sent.append(lax.ppermute(blocks, "dp", swap_core()))
    kept, arrived = [], []
    for s in range(STREAMS):
        own = outgoing_blocks(mine_to + s, bitmap, gradients, residual)
        parts = pair_sums(own, sent[s])
        arrived.append([lax.ppermute(parts[i], "dp", shift_first(SHIFTS[i])) for i in range(3)])
        kept.append(parts[3])
    new_residual = left_over(bitmap, gradients, residual)

    full, rows = [], []
    for s in range(STREAMS):
        part = block_sum(kept[s], *arrived[s])
        masks = (1, 3) if s == 0 else (3, 1)
        part = block_sum(part, lax.ppermute(part, "dp", swap_second(masks[0])))
        first = ((core * 8 + mine * 2 + s) * BLOCK).reshape(1)
        block, row = last_sum(first, table, part, lax.ppermute(part, "dp", swap_second(masks[1])))
        full.append(block)
        rows.append(row)

    gathered = []
    for s in range(STREAMS):
        gathered.append([lax.ppermute(full[s], "dp", shift_first(SHIFTS[i])) for i in range(3)])
        gathered[-1].append(full[s])
    row = rows[0] + rows[1]
    row = row_sum(row, [lax.ppermute(row, "tensor", shift_tensor(k)) for k in (1, 2, 3)])
    row = row_sum(row, [lax.ppermute(row, "dp", shift_first(k)) for k in (1, 2, 3)])
    other = lax.ppermute(row, "dp", swap_core())

    blocks, index = [], []
    for s in range(STREAMS):
        for i in range(4):
            blocks.append(gathered[s][i])
            index.append(mine_from[i] + s)
            blocks.append(lax.ppermute(gathered[s][i], "dp", swap_core()))
            index.append(theirs_from[i] + s)
    new_momentum = finish(jnp.stack(index), table, row, other, momentum, blocks)
    return (new_residual[None], new_momentum)


def solution(mesh):
    return jax.shard_map(
        shards,
        mesh=mesh,
        in_specs=(
            P("dp", "tensor", None, None),
            P("dp", "tensor", None, None),
            P("tensor", None, None),
            P("dp", "tensor"),
            P(),
        ),
        out_specs=(P("dp", "tensor", None, None), P("tensor", None, None)),
        check_vma=False,
    )
```

```python
import functools

import jax
import jax.numpy as jnp
from jax import lax
from jax.experimental import pallas as pl
from jax.experimental.pallas import tpu as pltpu
from jax.sharding import PartitionSpec as P

MOMENTUM = 0.9
CLIP_LEVEL = 3.0
EPSILON = 1e-06
BF16 = jnp.bfloat16
F32 = jnp.float32
HALF = 8
BLOCK = 16
GROUPS = ((2, 1), (3, 0))
RETURNED = (0, 1, 3, 2)
MIB = 2**20


def dp_index(z, x, core):
    return (z * 4 + x) * 2 + core


def each_dp():
    return [(d, d // 8, (d // 2) % 4, d % 2) for d in range(32)]


def swap_core():
    return [(d, d ^ 1) for d in range(32)]


def along(axis, move):
    pairs = []
    for d, z, x, core in each_dp():
        on_x = (core == 0) == (axis == 0)
        to = dp_index(z, move(x), core) if on_x else dp_index(move(z), x, core)
        pairs.append((d, to))
    return pairs


def shift_first(k):
    return along(0, lambda p: (p + k) % 4)


def swap_first(mask):
    return along(0, lambda p: p ^ mask)


def swap_second(mask):
    return along(1, lambda p: p ^ mask)


def swap_tensor(mask):
    return [(i, i ^ mask) for i in range(4)]


def after(array, earlier):
    return lax.optimization_barrier((array, earlier))[0]


def send(array, pairs, axis="dp"):
    return lax.ppermute(array, axis, pairs)


def places():
    dp = lax.axis_index("dp")
    z, x, core = lax.div(dp, 8), lax.rem(lax.div(dp, 2), 4), lax.rem(dp, 2)
    return core, jnp.where(core == 0, x, z), jnp.where(core == 0, z, x)


def block_of(side, shift):
    core, mine, theirs = places()
    if side:
        core, mine = 1 - core, theirs
    return core * 4 + lax.rem(mine + shift + 4, 4)


def spec_of(tiles, index_map):
    return pl.BlockSpec((tiles, 128, 128), index_map)


def tiles_shape(count):
    return jax.ShapeDtypeStruct((count, 128, 128), BF16)


def params(mib=40):
    return pltpu.CompilerParams(vmem_limit_bytes=mib * MIB)


def cost(tiles_read_or_written):
    return pl.CostEstimate(
        flops=tiles_read_or_written * 16384,
        bytes_accessed=tiles_read_or_written * 32768,
        transcendentals=0,
    )


def outgoing_kernel(side, shifts, bitmap_hbm, g_hbm, r_hbm, out_ref, bitmap, g_ref, r_ref, sems):
    firsts = [block_of(side, k) * BLOCK + h * HALF for k in shifts for h in range(2)]
    chosen = pltpu.make_async_copy(bitmap_hbm, bitmap, sems.at[0, 0])
    chosen.start()
    copies = []
    for i, first in enumerate(firsts):
        rows, place = pl.ds(first, HALF), pl.ds(i * HALF, HALF)
        for j, (source, target) in enumerate(((g_hbm, g_ref), (r_hbm, r_ref))):
            copy = pltpu.make_async_copy(source.at[rows], target.at[place], sems.at[i + 1, j])
            copy.start()
            copies.append(copy)
    chosen.wait()
    for i, first in enumerate(firsts):
        copies[2 * i].wait()
        copies[2 * i + 1].wait()
        for t in range(HALF):
            place = i * HALF + t
            value = (g_ref[place].astype(F32) + r_ref[place].astype(F32)).astype(BF16)
            out_ref[place] = jnp.where(bitmap[0, first + t] > 0, value, jnp.zeros_like(value))


def outgoing(side, shifts, bitmap, gradients, residual):
    tiles = len(shifts) * BLOCK
    return pl.pallas_call(
        functools.partial(outgoing_kernel, side, shifts),
        in_specs=[pl.BlockSpec(memory_space=pl.ANY)] * 3,
        out_specs=pl.BlockSpec(memory_space=pltpu.VMEM),
        out_shape=tiles_shape(tiles),
        scratch_shapes=[
            pltpu.SMEM((1, 128), jnp.int32),
            pltpu.VMEM((tiles, 128, 128), BF16),
            pltpu.VMEM((tiles, 128, 128), BF16),
            pltpu.SemaphoreType.DMA((2 * len(shifts) + 1, 2)),
        ],
        compiler_params=params(),
        cost_estimate=cost(3 * tiles),
    )(bitmap, gradients, residual)


def left_kernel(after_ref, bitmap_ref, g_ref, r_ref, out_ref, token_ref):
    first = pl.program_id(0) * BLOCK
    for t in range(BLOCK):
        value = (g_ref[t].astype(F32) + r_ref[t].astype(F32)).astype(BF16)
        out_ref[t] = jnp.where(bitmap_ref[0, first + t] > 0, jnp.zeros_like(value), value)
    token_ref[...] = jnp.zeros_like(token_ref)


def left_over(after, bitmap, gradients, residual):
    block = spec_of(BLOCK, lambda i: (i, 0, 0))
    return pl.pallas_call(
        left_kernel,
        grid=(8,),
        in_specs=[
            pl.BlockSpec(memory_space=pl.ANY),
            pl.BlockSpec(memory_space=pltpu.SMEM),
            block,
            block,
        ],
        out_specs=[block, pl.BlockSpec((8, 128), lambda i: (0, 0))],
        out_shape=[tiles_shape(128), jax.ShapeDtypeStruct((8, 128), F32)],
        compiler_params=params(),
        cost_estimate=cost(3 * 128),
    )(after, bitmap, gradients, residual)


def pair_kernel(a_ref, b_ref, *out_refs):
    for k, out_ref in enumerate(out_refs):

        @pl.when(pl.program_id(0) == k)
        def _():
            out_ref[...] = (a_ref[...].astype(F32) + b_ref[...].astype(F32)).astype(BF16)


def pair_sums(a, b):
    count = a.shape[0] // BLOCK
    return pl.pallas_call(
        pair_kernel,
        grid=(count,),
        in_specs=[spec_of(BLOCK, lambda i: (i, 0, 0))] * 2,
        out_specs=[spec_of(BLOCK, lambda i: (0, 0, 0))] * count,
        out_shape=[tiles_shape(BLOCK)] * count,
        compiler_params=params(),
        cost_estimate=cost(3 * count * BLOCK),
    )(a, b)


def total_kernel(after_ref, r0, r1, r2, r3, low_ref, high_ref):
    for t in range(BLOCK):
        total = (r0[t].astype(F32) + r2[t].astype(F32)) + (r1[t].astype(F32) + r3[t].astype(F32))
        out_ref = low_ref if t < HALF else high_ref
        out_ref[t % HALF] = total.astype(BF16)


def block_total(after, *blocks):
    return pl.pallas_call(
        total_kernel,
        in_specs=[pl.BlockSpec(memory_space=pl.ANY)] + [spec_of(BLOCK, lambda: (0, 0, 0))] * 4,
        out_specs=[spec_of(HALF, lambda: (0, 0, 0))] * 2,
        out_shape=[tiles_shape(HALF)] * 2,
        compiler_params=params(),
        cost_estimate=cost(5 * BLOCK),
    )(after, *blocks)


def halves_kernel(a0, a1, b0, b1, low_ref, high_ref):
    for t in range(HALF):
        low_ref[t] = (a0[t].astype(F32) + a1[t].astype(F32)).astype(BF16)
        high_ref[t] = (b0[t].astype(F32) + b1[t].astype(F32)).astype(BF16)


def halves_sum(*halves):
    return pl.pallas_call(
        halves_kernel,
        in_specs=[spec_of(HALF, lambda: (0, 0, 0))] * 4,
        out_specs=[spec_of(HALF, lambda: (0, 0, 0))] * 2,
        out_shape=[tiles_shape(HALF)] * 2,
        compiler_params=params(),
        cost_estimate=cost(6 * HALF),
    )(*halves)


def last_kernel(lo_ref, hi_ref, a0, a1, b0, b1, out_ref, row_ref):
    shard = lax.axis_index("tensor")
    lo, hi = lo_ref[pl.ds(shard, 1), :], hi_ref[pl.ds(shard, 1), :]
    first = block_of(0, 0) * BLOCK
    row = jnp.zeros((1, 128), F32)
    for t in range(BLOCK):
        left, right = (a0, a1) if t < HALF else (b0, b1)
        total = left[t % HALF].astype(F32) + right[t % HALF].astype(F32)
        out_ref[t] = total.astype(BF16)
        square = jnp.sum(jnp.sum(total * total, axis=0, keepdims=True), axis=1, keepdims=True)
        row = row + jnp.where((lo <= first + t) & (first + t < hi), square, 0.0)
    row_ref[...] = jnp.broadcast_to(row, (8, 128))


def last_sum(lo, hi, *halves):
    return pl.pallas_call(
        last_kernel,
        out_shape=[tiles_shape(BLOCK), jax.ShapeDtypeStruct((8, 128), F32)],
        compiler_params=params(),
        cost_estimate=cost(6 * HALF),
    )(lo, hi, *halves)


def final_kernel(lo_ref, hi_ref, mine_ref, other_ref, m_ref, *refs):
    blocks, (out_ref, factor_ref, ready_ref, sems) = refs[:8], refs[8:]
    shard = lax.axis_index("tensor")
    lo, hi = lo_ref[pl.ds(shard, 1), :], hi_ref[pl.ds(shard, 1), :]
    count = jnp.sum((hi_ref[...] - lo_ref[...]).astype(F32), axis=0, keepdims=True)
    squares = mine_ref[0:1, :] + other_ref[0:1, :]
    rms = jnp.sqrt(squares / (jnp.maximum(count, 1.0) * 16384.0) + EPSILON)
    clip = jnp.minimum(1.0, CLIP_LEVEL / rms)
    tile = lax.broadcasted_iota(jnp.int32, (128, 128), 0)
    chosen = jnp.where((lo <= tile) & (tile < hi), clip, 0.0)
    factor_ref[...] = jnp.broadcast_to(jnp.sum(chosen, axis=1, keepdims=True), (128, 128))

    copies = []
    for k, block in enumerate(blocks):
        first = block_of(k % 2, -RETURNED[k // 2]) * BLOCK

        def one_tile(t, carry):
            factor = factor_ref[pl.ds(first + t, 1), :]
            update = block[t].astype(F32) * factor
            new = MOMENTUM * m_ref[first + t].astype(F32) + update
            ready_ref[k * BLOCK + t] = new.astype(BF16)
            return carry

        lax.fori_loop(0, BLOCK, one_tile, 0, unroll=4)
        copies.append(
            pltpu.make_async_copy(
                ready_ref.at[pl.ds(k * BLOCK, BLOCK)],
                out_ref.at[pl.ds(first, BLOCK)],
                sems.at[k],
            )
        )
        copies[-1].start()
    for copy in copies:
        copy.wait()


def finish(lo, hi, mine, other, momentum, blocks):
    whole = pl.BlockSpec(memory_space=pltpu.VMEM)
    return pl.pallas_call(
        final_kernel,
        in_specs=[whole] * (5 + len(blocks)),
        out_specs=pl.BlockSpec(memory_space=pl.ANY),
        scratch_shapes=[
            pltpu.VMEM((128, 128), F32),
            pltpu.VMEM((128, 128, 128), BF16),
            pltpu.SemaphoreType.DMA((8,)),
        ],
        out_shape=tiles_shape(128),
        compiler_params=params(20),
        cost_estimate=cost(3 * 128),
    )(lo, hi, mine, other, momentum, *blocks)


def shards(gradients, residual, momentum, bitmap, starts):
    gradients, residual = gradients[0], residual[0]
    lo = jnp.pad(starts, ((0, 0), (0, 96)), constant_values=128)
    hi = jnp.pad(starts[:, 1:], ((0, 0), (0, 97)), constant_values=128)

    gradients = pltpu.with_memory_space_constraint(gradients, pltpu.HBM)
    residual = pltpu.with_memory_space_constraint(residual, pltpu.HBM)
    bitmap = pltpu.with_memory_space_constraint(bitmap, pltpu.HBM)
    arrays = (bitmap, gradients, residual)
    swapped = [send(outgoing(1, shifts, *arrays), swap_core()) for shifts in GROUPS]
    kept = [outgoing(0, shifts, *arrays) for shifts in GROUPS]
    first = pair_sums(kept[0], swapped[0])
    by_two = send(first[0], shift_first(2))
    by_one = send(first[1], shift_first(1))
    second = pair_sums(kept[1], swapped[1])
    by_three = send(second[0], shift_first(3))
    left, token = left_over(second[0], *arrays)

    low, high = block_total(token, second[1], by_one, by_two, by_three)
    low, high = halves_sum(low, send(low, swap_second(1)), high, send(high, swap_second(3)))
    full, row = last_sum(lo, hi, low, send(low, swap_second(3)), high, send(high, swap_second(1)))

    returned = {2: send(full, shift_first(2))}
    row = row + send(row, swap_tensor(1), "tensor")
    full = after(full, row)
    returned[1] = send(full, shift_first(1))
    row = row + send(row, swap_tensor(3), "tensor")
    full = after(full, row)
    returned[3] = send(full, shift_first(3))
    for mask in (1, 3):
        row = row + send(row, swap_first(mask))
    other = send(row, swap_core())

    blocks = [full, send(full, swap_core())]
    for k in RETURNED[1:]:
        blocks += [returned[k], send(after(returned[k], row), swap_core())]
    return (left[None], finish(lo, hi, row, other, momentum, blocks))


def solution(mesh):
    return jax.shard_map(
        shards,
        mesh=mesh,
        in_specs=(
            P("dp", "tensor", None, None),
            P("dp", "tensor", None, None),
            P("tensor", None, None),
            P("dp", "tensor"),
            P(),
        ),
        out_specs=(P("dp", "tensor", None, None), P("tensor", None, None)),
        check_vma=False,
    )
```

```python
import functools

import jax
import jax.numpy as jnp
from jax import lax
from jax.experimental import pallas as pl
from jax.experimental.pallas import tpu as pltpu
from jax.sharding import PartitionSpec as P

MOMENTUM = 0.9
CLIP_LEVEL = 3.0
EPSILON = 1e-06
BF16 = jnp.bfloat16
F32 = jnp.float32
HALF = 8
BLOCK = 16
ROWS = 16
CHAIN = 3
GROUPS = ((2, 1), (3, 0))
RETURNED = (0, 1, 3, 2)
MIB = 2**20


def dp_index(z, x, core):
    return (z * 4 + x) * 2 + core


def each_dp():
    return [(d, d // 8, (d // 2) % 4, d % 2) for d in range(32)]


def swap_core():
    return [(d, d ^ 1) for d in range(32)]


def along(axis, move):
    pairs = []
    for d, z, x, core in each_dp():
        on_x = (core == 0) == (axis == 0)
        to = dp_index(z, move(x), core) if on_x else dp_index(move(z), x, core)
        pairs.append((d, to))
    return pairs


def shift_first(k):
    return along(0, lambda p: (p + k) % 4)


def swap_second(mask):
    return along(1, lambda p: p ^ mask)


def swap_tensor(mask):
    return [(i, i ^ mask) for i in range(4)]


def after(array, earlier):
    return lax.optimization_barrier((array, earlier))[0]


def send(array, pairs, axis="dp"):
    return lax.ppermute(array, axis, pairs)


def places():
    dp = lax.axis_index("dp")
    z, x, core = lax.div(dp, 8), lax.rem(lax.div(dp, 2), 4), lax.rem(dp, 2)
    return core, jnp.where(core == 0, x, z), jnp.where(core == 0, z, x)


def block_of(side, shift):
    core, mine, theirs = places()
    if side:
        core, mine = 1 - core, theirs
    return core * 4 + lax.rem(mine + shift + 4, 4)


def spec_of(tiles, index_map):
    return pl.BlockSpec((tiles, 128, 128), index_map)


def tiles_shape(count):
    return jax.ShapeDtypeStruct((count, 128, 128), BF16)


def params(mib=40):
    return pltpu.CompilerParams(vmem_limit_bytes=mib * MIB)


def cost(tiles_read_or_written):
    return pl.CostEstimate(
        flops=tiles_read_or_written * 16384,
        bytes_accessed=tiles_read_or_written * 32768,
        transcendentals=0,
    )


def outgoing_kernel(side, shifts, outs_count, bitmap_hbm, g_hbm, r_hbm, *refs):
    given, outs, (bitmap, g_ref, r_ref, sems) = refs[:-5], refs[-5:-4], refs[-4:]
    if outs_count > 1:
        given, outs = refs[:1], refs[1:-4]
    firsts = [block_of(side, k) * BLOCK + h * HALF for k in shifts for h in range(2)]
    chosen = pltpu.make_async_copy(bitmap_hbm, bitmap, sems.at[0, 0])
    chosen.start()
    copies = []
    for i, first in enumerate(firsts):
        rows, place = pl.ds(first, HALF), pl.ds(i * HALF, HALF)
        for j, (source, target) in enumerate(((g_hbm, g_ref), (r_hbm, r_ref))):
            copy = pltpu.make_async_copy(source.at[rows], target.at[place], sems.at[i + 1, j])
            copy.start()
            copies.append(copy)
    chosen.wait()
    for i, first in enumerate(firsts):
        copies[2 * i].wait()
        copies[2 * i + 1].wait()
        for t in range(HALF):
            place = i * HALF + t
            value = g_ref[place] + r_ref[place]
            value = jnp.where(bitmap[0, first + t] > 0, value, jnp.zeros_like(value))
            if given:
                value = value + given[0][place]
                outs[place // BLOCK][place % BLOCK] = value
            else:
                outs[0][place] = value


def outgoing(side, shifts, bitmap, gradients, residual, *swapped):
    tiles = len(shifts) * BLOCK
    vmem = pl.BlockSpec(memory_space=pltpu.VMEM)
    shapes = [tiles_shape(BLOCK)] * len(shifts) if swapped else [tiles_shape(tiles)]
    return pl.pallas_call(
        functools.partial(outgoing_kernel, side, shifts, len(shapes)),
        in_specs=[pl.BlockSpec(memory_space=pl.ANY)] * 3 + [vmem] * len(swapped),
        out_specs=[vmem] * len(shapes),
        out_shape=shapes,
        scratch_shapes=[
            pltpu.SMEM((1, 128), jnp.int32),
            pltpu.VMEM((tiles, 128, 128), BF16),
            pltpu.VMEM((tiles, 128, 128), BF16),
            pltpu.SemaphoreType.DMA((2 * len(shifts) + 1, 2)),
        ],
        compiler_params=params(),
        cost_estimate=cost(3 * tiles),
    )(bitmap, gradients, residual, *swapped)


def left_kernel(after_ref, bitmap_ref, g_ref, r_ref, out_ref, token_ref):
    first = pl.program_id(0) * BLOCK
    for t in range(BLOCK):
        value = g_ref[t] + r_ref[t]
        out_ref[t] = jnp.where(bitmap_ref[0, first + t] > 0, jnp.zeros_like(value), value)
    token_ref[...] = jnp.zeros_like(token_ref)


def left_over(after, bitmap, gradients, residual):
    block = spec_of(BLOCK, lambda i: (i, 0, 0))
    return pl.pallas_call(
        left_kernel,
        grid=(8,),
        in_specs=[
            pl.BlockSpec(memory_space=pl.ANY),
            pl.BlockSpec(memory_space=pltpu.SMEM),
            block,
            block,
        ],
        out_specs=[block, pl.BlockSpec((8, 128), lambda i: (0, 0))],
        out_shape=[tiles_shape(128), jax.ShapeDtypeStruct((8, 128), F32)],
        compiler_params=params(),
        cost_estimate=cost(3 * 128),
    )(after, bitmap, gradients, residual)


def pair_kernel(a_ref, b_ref, *out_refs):
    for k, out_ref in enumerate(out_refs):

        @pl.when(pl.program_id(0) == k)
        def _():
            out_ref[...] = a_ref[...] + b_ref[...]


def pair_sums(a, b):
    count = a.shape[0] // BLOCK
    return pl.pallas_call(
        pair_kernel,
        grid=(count,),
        in_specs=[spec_of(BLOCK, lambda i: (i, 0, 0))] * 2,
        out_specs=[spec_of(BLOCK, lambda i: (0, 0, 0))] * count,
        out_shape=[tiles_shape(BLOCK)] * count,
        compiler_params=params(),
        cost_estimate=cost(3 * count * BLOCK),
    )(a, b)


def total_kernel(after_ref, r0, r1, r2, r3, low_ref, high_ref):
    for t in range(BLOCK):
        total = (r0[t].astype(F32) + r2[t].astype(F32)) + (r1[t].astype(F32) + r3[t].astype(F32))
        out_ref = low_ref if t < HALF else high_ref
        out_ref[t % HALF] = total.astype(BF16)


def block_total(after, *blocks):
    return pl.pallas_call(
        total_kernel,
        in_specs=[pl.BlockSpec(memory_space=pl.ANY)] + [spec_of(BLOCK, lambda: (0, 0, 0))] * 4,
        out_specs=[spec_of(HALF, lambda: (0, 0, 0))] * 2,
        out_shape=[tiles_shape(HALF)] * 2,
        compiler_params=params(),
        cost_estimate=cost(5 * BLOCK),
    )(after, *blocks)


def halves_kernel(a0, a1, b0, b1, low_ref, high_ref):
    for t in range(HALF):
        low_ref[t] = a0[t] + a1[t]
        high_ref[t] = b0[t] + b1[t]


def halves_sum(*halves):
    return pl.pallas_call(
        halves_kernel,
        in_specs=[spec_of(HALF, lambda: (0, 0, 0))] * 4,
        out_specs=[spec_of(HALF, lambda: (0, 0, 0))] * 2,
        out_shape=[tiles_shape(HALF)] * 2,
        compiler_params=params(),
        cost_estimate=cost(6 * HALF),
    )(*halves)


def put_tile(ref, t, value):
    ref[pl.ds(t * 128, 128), :] = value


def last_kernel(lo_ref, hi_ref, a0, a1, b0, b1, plain_ref, full_ref, row_ref):
    shard = lax.axis_index("tensor")
    lo, hi = lo_ref[pl.ds(shard, 1), :], hi_ref[pl.ds(shard, 1), :]
    first = block_of(0, 0) * BLOCK
    row = jnp.zeros((1, 128), F32)
    for t in range(BLOCK):
        left, right = (a0, a1) if t < HALF else (b0, b1)
        total = left[t % HALF].astype(F32) + right[t % HALF].astype(F32)
        put_tile(plain_ref, t, total.astype(BF16))
        put_tile(full_ref, t, total.astype(BF16))
        square = jnp.sum(jnp.sum(total * total, axis=0, keepdims=True), axis=1, keepdims=True)
        row = row + jnp.where((lo <= first + t) & (first + t < hi), square, 0.0)
    row_ref[...] = jnp.broadcast_to(row, (8, 128))


def flat_shape(tiles, rows):
    return jax.ShapeDtypeStruct((tiles * 128 + rows, 128), BF16)


def last_sum(lo, hi, *halves):
    return pl.pallas_call(
        last_kernel,
        out_shape=[
            flat_shape(BLOCK, 0),
            flat_shape(BLOCK, ROWS),
            jax.ShapeDtypeStruct((8, 128), F32),
        ],
        compiler_params=params(),
        cost_estimate=cost(6 * HALF),
    )(lo, hi, *halves)


def pack_kernel(full_ref, mine_ref, other_ref, out_ref, row_ref, sem):
    row = 0.5 * (mine_ref[0:1, :] + other_ref[0:1, :])
    rest, rows = jnp.broadcast_to(row, (ROWS, 128)), jnp.zeros((ROWS, 128), F32)
    place = lax.broadcasted_iota(jnp.int32, (ROWS, 128), 0)
    for i in range(3):
        part = rest.astype(BF16).astype(F32)
        rows = jnp.where(place == i, part, rows)
        rest = jnp.where(jnp.abs(part) < jnp.inf, rest - part, 0.0)
    row_ref[...] = rows.astype(BF16)
    copy = pltpu.make_async_copy(row_ref, out_ref.at[pl.ds(BLOCK * 128, ROWS), :], sem)
    copy.start()
    copy.wait()


def pack(full, mine, other):
    vmem = pl.BlockSpec(memory_space=pltpu.VMEM)
    anywhere = pl.BlockSpec(memory_space=pl.ANY)
    return pl.pallas_call(
        pack_kernel,
        in_specs=[anywhere, vmem, vmem],
        out_specs=[anywhere, vmem],
        out_shape=[flat_shape(BLOCK, ROWS), flat_shape(0, ROWS)],
        scratch_shapes=[pltpu.SemaphoreType.DMA],
        input_output_aliases={0: 0},
        compiler_params=params(),
        cost_estimate=cost(1),
    )(full, mine, other)


def rows_kernel(r0, r2, r1, r3, out_ref):
    rows = []
    for ref in (r0, r2, r1, r3):
        parts = ref[pl.ds(ref.shape[0] - ROWS, ROWS), :].astype(F32)
        rows.append((parts[0:1, :] + parts[1:2, :]) + parts[2:3, :])
    total = 2.0 * ((rows[0] + rows[1]) + (rows[2] + rows[3]))
    out_ref[...] = jnp.broadcast_to(total, (8, 128))


def sum_of_rows(*smalls):
    return pl.pallas_call(
        rows_kernel,
        out_shape=jax.ShapeDtypeStruct((8, 128), F32),
        compiler_params=params(),
        cost_estimate=cost(1),
    )(*smalls)


def final_kernel(lo_ref, hi_ref, mine_ref, other_ref, m_ref, *refs):
    blocks, (out_ref, factor_ref, ready_ref, sems) = refs[:8], refs[9:]
    shard = lax.axis_index("tensor")
    lo, hi = lo_ref[pl.ds(shard, 1), :], hi_ref[pl.ds(shard, 1), :]
    count = jnp.sum((hi_ref[...] - lo_ref[...]).astype(F32), axis=0, keepdims=True)
    squares = mine_ref[0:1, :] + other_ref[0:1, :]
    rms = jnp.sqrt(squares / (jnp.maximum(count, 1.0) * 16384.0) + EPSILON)
    clip = jnp.minimum(1.0, CLIP_LEVEL / rms)
    tile = lax.broadcasted_iota(jnp.int32, (128, 128), 0)
    chosen = jnp.where((lo <= tile) & (tile < hi), clip, 0.0)
    factor_ref[...] = jnp.broadcast_to(jnp.sum(chosen, axis=1, keepdims=True), (128, 128))

    def tiles_of(source, count, first, place):
        def one_tile(t, carry):
            value = source[pl.ds(pl.multiple_of(t * 128, 128), 128), :]
            update = value.astype(F32) * factor_ref[pl.ds(first + t, 1), :]
            new = MOMENTUM * m_ref[first + t].astype(F32) + update
            ready_ref[place + t] = new.astype(BF16)
            return carry

        lax.fori_loop(0, count, one_tile, 0, unroll=4)

    copies = []
    for k in range(8):
        first = block_of(k % 2, -RETURNED[k // 2]) * BLOCK
        tiles_of(blocks[k], BLOCK, first, k * BLOCK)
        copies.append(
            pltpu.make_async_copy(
                ready_ref.at[pl.ds(k * BLOCK, BLOCK)],
                out_ref.at[pl.ds(first, BLOCK)],
                sems.at[k],
            )
        )
        copies[-1].start()
    for copy in copies:
        copy.wait()


def finish(lo, hi, mine, other, momentum, blocks):
    whole = pl.BlockSpec(memory_space=pltpu.VMEM)
    return pl.pallas_call(
        final_kernel,
        in_specs=[whole] * (5 + len(blocks)),
        out_specs=pl.BlockSpec(memory_space=pl.ANY),
        scratch_shapes=[
            pltpu.VMEM((128, 128), F32),
            pltpu.VMEM((128, 128, 128), BF16),
            pltpu.SemaphoreType.DMA((8,)),
        ],
        out_shape=tiles_shape(128),
        compiler_params=params(20),
        cost_estimate=cost(3 * 128),
    )(lo, hi, mine, other, momentum, *blocks)


def shards(gradients, residual, momentum, bitmap, starts):
    gradients, residual = gradients[0], residual[0]
    lo = jnp.pad(starts, ((0, 0), (0, 96)), constant_values=128)
    hi = jnp.pad(starts[:, 1:], ((0, 0), (0, 97)), constant_values=128)

    gradients = pltpu.with_memory_space_constraint(gradients, pltpu.HBM)
    residual = pltpu.with_memory_space_constraint(residual, pltpu.HBM)
    bitmap = pltpu.with_memory_space_constraint(bitmap, pltpu.HBM)
    arrays = (bitmap, gradients, residual)
    swapped = [send(outgoing(1, shifts, *arrays)[0], swap_core()) for shifts in GROUPS]
    two, one = pair_sums(outgoing(0, GROUPS[0], *arrays)[0], swapped[0])
    by_two, by_one = send(two, shift_first(2)), send(one, shift_first(1))
    three, own = outgoing(0, GROUPS[1], *arrays, swapped[1])
    by_three = send(three, shift_first(3))
    left, token = left_over(three, *arrays)

    low, high = block_total(token, own, by_one, by_two, by_three)
    low, high = halves_sum(low, send(low, swap_second(1)), high, send(high, swap_second(3)))
    plain, full, row = last_sum(
        lo, hi, low, send(low, swap_second(3)), high, send(high, swap_second(1))
    )

    by_two = send(plain, shift_first(2))
    row = row + send(row, swap_tensor(1), "tensor")
    full, row = pack(full, row, send(row, swap_tensor(3), "tensor"))
    by_one, by_three = send(full, shift_first(1)), send(full, shift_first(3))
    row_two = send(row, shift_first(2))
    row = sum_of_rows(full, row_two, by_one, by_three)
    other = send(row, swap_core())
    blocks = [full, send(full, swap_core())]
    for block in (after(by_one, row_two), by_three):
        blocks += [block, send(block, swap_core())]
    token = by_two[:ROWS]
    for _ in range(CHAIN):
        token = send(token, swap_core())
    moved, token = lax.optimization_barrier((by_two, token))
    blocks += [by_two, send(moved, swap_core()), token]
    return (left[None], finish(lo, hi, row, other, momentum, blocks))


def solution(mesh):
    return jax.shard_map(
        shards,
        mesh=mesh,
        in_specs=(
            P("dp", "tensor", None, None),
            P("dp", "tensor", None, None),
            P("tensor", None, None),
            P("dp", "tensor"),
            P(),
        ),
        out_specs=(P("dp", "tensor", None, None), P("tensor", None, None)),
        check_vma=False,
    )
```

```python
import functools

import jax
import jax.numpy as jnp
from jax import lax
from jax.experimental import pallas as pl
from jax.experimental.pallas import tpu as pltpu
from jax.sharding import PartitionSpec as P

MOMENTUM = 0.9
CLIP_LEVEL = 3.0
EPSILON = 1e-06
BF16 = jnp.bfloat16
F32 = jnp.float32
HALF = 8
BLOCK = 16
ROWS = 16
CHAIN = 3
GROUPS = ((2, 1), (3, 0))
RETURNED = (0, 1, 3, 2)
MIB = 2**20


def dp_index(z, x, core):
    return (z * 4 + x) * 2 + core


def each_dp():
    return [(d, d // 8, (d // 2) % 4, d % 2) for d in range(32)]


def swap_core():
    return [(d, d ^ 1) for d in range(32)]


def along(axis, move):
    pairs = []
    for d, z, x, core in each_dp():
        on_x = (core == 0) == (axis == 0)
        to = dp_index(z, move(x), core) if on_x else dp_index(move(z), x, core)
        pairs.append((d, to))
    return pairs


def shift_first(k):
    return along(0, lambda p: (p + k) % 4)


def swap_second(mask):
    return along(1, lambda p: p ^ mask)


def swap_tensor(mask):
    return [(i, i ^ mask) for i in range(4)]


def after(array, earlier):
    return lax.optimization_barrier((array, earlier))[0]


def send(array, pairs, axis="dp"):
    return lax.ppermute(array, axis, pairs)


def places():
    dp = lax.axis_index("dp")
    z, x, core = lax.div(dp, 8), lax.rem(lax.div(dp, 2), 4), lax.rem(dp, 2)
    return core, jnp.where(core == 0, x, z), jnp.where(core == 0, z, x)


def block_of(side, shift):
    core, mine, theirs = places()
    if side:
        core, mine = 1 - core, theirs
    return core * 4 + lax.rem(mine + shift + 4, 4)


def spec_of(tiles, index_map):
    return pl.BlockSpec((tiles, 128, 128), index_map)


def tiles_shape(count):
    return jax.ShapeDtypeStruct((count, 128, 128), BF16)


def params(mib=40):
    return pltpu.CompilerParams(vmem_limit_bytes=mib * MIB)


def cost(tiles_read_or_written):
    return pl.CostEstimate(
        flops=tiles_read_or_written * 16384,
        bytes_accessed=tiles_read_or_written * 32768,
        transcendentals=0,
    )


def outgoing_kernel(side, bitmap_hbm, g_hbm, r_hbm, *refs):
    outs, (bitmap, g_ref, r_ref, sems) = refs[:2], refs[2:]
    shifts = [k for group in GROUPS for k in group]
    firsts = [block_of(side, k) * BLOCK + h * HALF for k in shifts for h in range(2)]
    chosen = pltpu.make_async_copy(bitmap_hbm, bitmap, sems.at[0, 0])
    chosen.start()
    copies = []
    for i, first in enumerate(firsts):
        rows, place = pl.ds(first, HALF), pl.ds(i * HALF, HALF)
        for j, (source, target) in enumerate(((g_hbm, g_ref), (r_hbm, r_ref))):
            copy = pltpu.make_async_copy(source.at[rows], target.at[place], sems.at[i + 1, j])
            copy.start()
            copies.append(copy)
    chosen.wait()
    for i, first in enumerate(firsts):
        copies[2 * i].wait()
        copies[2 * i + 1].wait()
        for t in range(HALF):
            place = i * HALF + t
            value = g_ref[place] + r_ref[place]
            value = jnp.where(bitmap[0, first + t] > 0, value, jnp.zeros_like(value))
            outs[place // (2 * BLOCK)][place % (2 * BLOCK)] = value


def outgoing(side, bitmap, gradients, residual):
    vmem = pl.BlockSpec(memory_space=pltpu.VMEM)
    return pl.pallas_call(
        functools.partial(outgoing_kernel, side),
        in_specs=[pl.BlockSpec(memory_space=pl.ANY)] * 3,
        out_specs=[vmem] * 2,
        out_shape=[tiles_shape(2 * BLOCK)] * 2,
        scratch_shapes=[
            pltpu.SMEM((1, 128), jnp.int32),
            pltpu.VMEM((4 * BLOCK, 128, 128), BF16),
            pltpu.VMEM((4 * BLOCK, 128, 128), BF16),
            pltpu.SemaphoreType.DMA((9, 2)),
        ],
        compiler_params=params(),
        cost_estimate=cost(12 * BLOCK),
    )(bitmap, gradients, residual)


def left_kernel(after_ref, bitmap_ref, g_ref, r_ref, out_ref, token_ref):
    first = pl.program_id(0) * BLOCK
    for t in range(BLOCK):
        value = g_ref[t] + r_ref[t]
        out_ref[t] = jnp.where(bitmap_ref[0, first + t] > 0, jnp.zeros_like(value), value)
    token_ref[...] = jnp.zeros_like(token_ref)


def left_over(after, bitmap, gradients, residual):
    block = spec_of(BLOCK, lambda i: (i, 0, 0))
    return pl.pallas_call(
        left_kernel,
        grid=(8,),
        in_specs=[
            pl.BlockSpec(memory_space=pl.ANY),
            pl.BlockSpec(memory_space=pltpu.SMEM),
            block,
            block,
        ],
        out_specs=[block, pl.BlockSpec((8, 128), lambda i: (0, 0))],
        out_shape=[tiles_shape(128), jax.ShapeDtypeStruct((8, 128), F32)],
        compiler_params=params(),
        cost_estimate=cost(3 * 128),
    )(after, bitmap, gradients, residual)


def pair_kernel(a_ref, b_ref, *out_refs):
    for k, out_ref in enumerate(out_refs):

        @pl.when(pl.program_id(0) == k)
        def _():
            out_ref[...] = a_ref[...] + b_ref[...]


def pair_sums(a, b):
    count = a.shape[0] // BLOCK
    return pl.pallas_call(
        pair_kernel,
        grid=(count,),
        in_specs=[spec_of(BLOCK, lambda i: (i, 0, 0))] * 2,
        out_specs=[spec_of(BLOCK, lambda i: (0, 0, 0))] * count,
        out_shape=[tiles_shape(BLOCK)] * count,
        compiler_params=params(),
        cost_estimate=cost(3 * count * BLOCK),
    )(a, b)


def total_kernel(after_ref, r0, r1, r2, r3, low_ref, high_ref):
    for t in range(BLOCK):
        total = (r0[t].astype(F32) + r2[t].astype(F32)) + (r1[t].astype(F32) + r3[t].astype(F32))
        out_ref = low_ref if t < HALF else high_ref
        out_ref[t % HALF] = total.astype(BF16)


def block_total(after, *blocks):
    return pl.pallas_call(
        total_kernel,
        in_specs=[pl.BlockSpec(memory_space=pl.ANY)] + [spec_of(BLOCK, lambda: (0, 0, 0))] * 4,
        out_specs=[spec_of(HALF, lambda: (0, 0, 0))] * 2,
        out_shape=[tiles_shape(HALF)] * 2,
        compiler_params=params(),
        cost_estimate=cost(5 * BLOCK),
    )(after, *blocks)


def halves_kernel(a0, a1, b0, b1, low_ref, high_ref):
    for t in range(HALF):
        low_ref[t] = a0[t] + a1[t]
        high_ref[t] = b0[t] + b1[t]


def halves_sum(*halves):
    return pl.pallas_call(
        halves_kernel,
        in_specs=[spec_of(HALF, lambda: (0, 0, 0))] * 4,
        out_specs=[spec_of(HALF, lambda: (0, 0, 0))] * 2,
        out_shape=[tiles_shape(HALF)] * 2,
        compiler_params=params(),
        cost_estimate=cost(6 * HALF),
    )(*halves)


def put_tile(ref, t, value):
    ref[pl.ds(t * 128, 128), :] = value


def last_kernel(lo_ref, hi_ref, a0, a1, b0, b1, plain_ref, full_ref, row_ref):
    shard = lax.axis_index("tensor")
    lo, hi = lo_ref[pl.ds(shard, 1), :], hi_ref[pl.ds(shard, 1), :]
    first = block_of(0, 0) * BLOCK
    row = jnp.zeros((1, 128), F32)
    for t in range(BLOCK):
        left, right = (a0, a1) if t < HALF else (b0, b1)
        total = left[t % HALF].astype(F32) + right[t % HALF].astype(F32)
        put_tile(plain_ref, t, total.astype(BF16))
        put_tile(full_ref, t, total.astype(BF16))
        square = jnp.sum(jnp.sum(total * total, axis=0, keepdims=True), axis=1, keepdims=True)
        row = row + jnp.where((lo <= first + t) & (first + t < hi), square, 0.0)
    row_ref[...] = jnp.broadcast_to(row, (8, 128))


def flat_shape(tiles, rows):
    return jax.ShapeDtypeStruct((tiles * 128 + rows, 128), BF16)


def last_sum(lo, hi, *halves):
    return pl.pallas_call(
        last_kernel,
        out_shape=[
            flat_shape(BLOCK, 0),
            flat_shape(BLOCK, ROWS),
            jax.ShapeDtypeStruct((8, 128), F32),
        ],
        compiler_params=params(),
        cost_estimate=cost(6 * HALF),
    )(lo, hi, *halves)


def pack_kernel(full_ref, mine_ref, other_ref, out_ref, row_ref, sem):
    row = 0.5 * (mine_ref[0:1, :] + other_ref[0:1, :])
    rest, rows = jnp.broadcast_to(row, (ROWS, 128)), jnp.zeros((ROWS, 128), F32)
    place = lax.broadcasted_iota(jnp.int32, (ROWS, 128), 0)
    for i in range(3):
        part = rest.astype(BF16).astype(F32)
        rows = jnp.where(place == i, part, rows)
        rest = jnp.where(jnp.abs(part) < jnp.inf, rest - part, 0.0)
    row_ref[...] = rows.astype(BF16)
    copy = pltpu.make_async_copy(row_ref, out_ref.at[pl.ds(BLOCK * 128, ROWS), :], sem)
    copy.start()
    copy.wait()


def pack(full, mine, other):
    vmem = pl.BlockSpec(memory_space=pltpu.VMEM)
    anywhere = pl.BlockSpec(memory_space=pl.ANY)
    return pl.pallas_call(
        pack_kernel,
        in_specs=[anywhere, vmem, vmem],
        out_specs=[anywhere, vmem],
        out_shape=[flat_shape(BLOCK, ROWS), flat_shape(0, ROWS)],
        scratch_shapes=[pltpu.SemaphoreType.DMA],
        input_output_aliases={0: 0},
        compiler_params=params(),
        cost_estimate=cost(1),
    )(full, mine, other)


def rows_kernel(r0, r2, r1, r3, out_ref):
    rows = []
    for ref in (r0, r2, r1, r3):
        parts = ref[pl.ds(ref.shape[0] - ROWS, ROWS), :].astype(F32)
        rows.append((parts[0:1, :] + parts[1:2, :]) + parts[2:3, :])
    total = 2.0 * ((rows[0] + rows[1]) + (rows[2] + rows[3]))
    out_ref[...] = jnp.broadcast_to(total, (8, 128))


def sum_of_rows(*smalls):
    return pl.pallas_call(
        rows_kernel,
        out_shape=jax.ShapeDtypeStruct((8, 128), F32),
        compiler_params=params(),
        cost_estimate=cost(1),
    )(*smalls)


def final_kernel(lo_ref, hi_ref, mine_ref, other_ref, m_ref, *refs):
    blocks, (out_ref, factor_ref, ready_ref, sems) = refs[:8], refs[9:]
    shard = lax.axis_index("tensor")
    lo, hi = lo_ref[pl.ds(shard, 1), :], hi_ref[pl.ds(shard, 1), :]
    count = jnp.sum((hi_ref[...] - lo_ref[...]).astype(F32), axis=0, keepdims=True)
    squares = mine_ref[0:1, :] + other_ref[0:1, :]
    rms = jnp.sqrt(squares / (jnp.maximum(count, 1.0) * 16384.0) + EPSILON)
    clip = jnp.minimum(1.0, CLIP_LEVEL / rms)
    tile = lax.broadcasted_iota(jnp.int32, (128, 128), 0)
    chosen = jnp.where((lo <= tile) & (tile < hi), clip, 0.0)
    factor_ref[...] = jnp.broadcast_to(jnp.sum(chosen, axis=1, keepdims=True), (128, 128))

    def tiles_of(source, count, first, place):
        def one_tile(t, carry):
            value = source[pl.ds(pl.multiple_of(t * 128, 128), 128), :]
            update = value.astype(F32) * factor_ref[pl.ds(first + t, 1), :]
            new = MOMENTUM * m_ref[first + t].astype(F32) + update
            ready_ref[place + t] = new.astype(BF16)
            return carry

        lax.fori_loop(0, count, one_tile, 0, unroll=4)

    copies = []
    for k in range(8):
        first = block_of(k % 2, -RETURNED[k // 2]) * BLOCK
        tiles_of(blocks[k], BLOCK, first, k * BLOCK)
        copies.append(
            pltpu.make_async_copy(
                ready_ref.at[pl.ds(k * BLOCK, BLOCK)],
                out_ref.at[pl.ds(first, BLOCK)],
                sems.at[k],
            )
        )
        copies[-1].start()
    for copy in copies:
        copy.wait()


def finish(lo, hi, mine, other, momentum, blocks):
    whole = pl.BlockSpec(memory_space=pltpu.VMEM)
    return pl.pallas_call(
        final_kernel,
        in_specs=[whole] * (5 + len(blocks)),
        out_specs=pl.BlockSpec(memory_space=pl.ANY),
        scratch_shapes=[
            pltpu.VMEM((128, 128), F32),
            pltpu.VMEM((128, 128, 128), BF16),
            pltpu.SemaphoreType.DMA((8,)),
        ],
        out_shape=tiles_shape(128),
        compiler_params=params(20),
        cost_estimate=cost(3 * 128),
    )(lo, hi, mine, other, momentum, *blocks)


def shards(gradients, residual, momentum, bitmap, starts):
    gradients, residual = gradients[0], residual[0]
    lo = jnp.pad(starts, ((0, 0), (0, 96)), constant_values=128)
    hi = jnp.pad(starts[:, 1:], ((0, 0), (0, 97)), constant_values=128)

    gradients = pltpu.with_memory_space_constraint(gradients, pltpu.HBM)
    residual = pltpu.with_memory_space_constraint(residual, pltpu.HBM)
    bitmap = pltpu.with_memory_space_constraint(bitmap, pltpu.HBM)
    arrays = (bitmap, gradients, residual)
    swapped = [send(part, swap_core()) for part in outgoing(1, *arrays)]
    kept = outgoing(0, *arrays)
    two, one = pair_sums(kept[0], swapped[0])
    by_two, by_one = send(two, shift_first(2)), send(one, shift_first(1))
    three, own = pair_sums(kept[1], swapped[1])
    by_three = send(three, shift_first(3))
    left, token = left_over(three, *arrays)

    low, high = block_total(token, own, by_one, by_two, by_three)
    low, high = halves_sum(low, send(low, swap_second(1)), high, send(high, swap_second(3)))
    plain, full, row = last_sum(
        lo, hi, low, send(low, swap_second(3)), high, send(high, swap_second(1))
    )

    by_two = send(plain, shift_first(2))
    row = row + send(row, swap_tensor(1), "tensor")
    full, row = pack(full, row, send(row, swap_tensor(3), "tensor"))
    by_one, by_three = send(full, shift_first(1)), send(full, shift_first(3))
    row_two = send(row, shift_first(2))
    row = sum_of_rows(full, row_two, by_one, by_three)
    other = send(row, swap_core())
    blocks = [full, send(full, swap_core())]
    for block in (after(by_one, row_two), by_three):
        blocks += [block, send(block, swap_core())]
    token = by_two[:ROWS]
    for _ in range(CHAIN):
        token = send(token, swap_core())
    moved, token = lax.optimization_barrier((by_two, token))
    blocks += [by_two, send(moved, swap_core()), token]
    return (left[None], finish(lo, hi, row, other, momentum, blocks))


def solution(mesh):
    return jax.shard_map(
        shards,
        mesh=mesh,
        in_specs=(
            P("dp", "tensor", None, None),
            P("dp", "tensor", None, None),
            P("tensor", None, None),
            P("dp", "tensor"),
            P(),
        ),
        out_specs=(P("dp", "tensor", None, None), P("tensor", None, None)),
        check_vma=False,
    )
```

```python
import functools

import jax
import jax.numpy as jnp
from jax import lax
from jax.experimental import pallas as pl
from jax.experimental.pallas import tpu as pltpu
from jax.sharding import PartitionSpec as P

MOMENTUM = 0.9
CLIP_LEVEL = 3.0
EPSILON = 1e-06
BF16 = jnp.bfloat16
F32 = jnp.float32
HALF = 8
BLOCK = 16
ROWS = 16
CHAIN = 3
GROUPS = ((1, 3), (2, 0))
RETURNED = (0, 1, 3, 2)
MIB = 2**20


def dp_index(z, x, core):
    return (z * 4 + x) * 2 + core


def each_dp():
    return [(d, d // 8, (d // 2) % 4, d % 2) for d in range(32)]


def swap_core():
    return [(d, d ^ 1) for d in range(32)]


def along(axis, move):
    pairs = []
    for d, z, x, core in each_dp():
        on_x = (core == 0) == (axis == 0)
        to = dp_index(z, move(x), core) if on_x else dp_index(move(z), x, core)
        pairs.append((d, to))
    return pairs


def shift_first(k):
    return along(0, lambda p: (p + k) % 4)


def swap_second(mask):
    return along(1, lambda p: p ^ mask)


def swap_tensor(mask):
    return [(i, i ^ mask) for i in range(4)]


def after(array, earlier):
    return lax.optimization_barrier((array, earlier))[0]


def send(array, pairs, axis="dp"):
    return lax.ppermute(array, axis, pairs)


def places():
    dp = lax.axis_index("dp")
    z, x, core = lax.div(dp, 8), lax.rem(lax.div(dp, 2), 4), lax.rem(dp, 2)
    return core, jnp.where(core == 0, x, z), jnp.where(core == 0, z, x)


def block_of(side, shift):
    core, mine, theirs = places()
    if side:
        core, mine = 1 - core, theirs
    return core * 4 + lax.rem(mine + shift + 4, 4)


def spec_of(tiles, index_map):
    return pl.BlockSpec((tiles, 128, 128), index_map)


def tiles_shape(count):
    return jax.ShapeDtypeStruct((count, 128, 128), BF16)


def params(mib=40):
    return pltpu.CompilerParams(vmem_limit_bytes=mib * MIB)


def cost(tiles_read_or_written):
    return pl.CostEstimate(
        flops=tiles_read_or_written * 16384,
        bytes_accessed=tiles_read_or_written * 32768,
        transcendentals=0,
    )


def outgoing_kernel(side, bitmap_hbm, g_hbm, r_hbm, *refs):
    outs, (bitmap, g_ref, r_ref, sems) = refs[:2], refs[2:]
    shifts = [k for group in GROUPS for k in group]
    firsts = [block_of(side, k) * BLOCK + h * HALF for k in shifts for h in range(2)]
    chosen = pltpu.make_async_copy(bitmap_hbm, bitmap, sems.at[0, 0])
    chosen.start()
    copies = []
    for i, first in enumerate(firsts):
        rows, place = pl.ds(first, HALF), pl.ds(i * HALF, HALF)
        for j, (source, target) in enumerate(((g_hbm, g_ref), (r_hbm, r_ref))):
            copy = pltpu.make_async_copy(source.at[rows], target.at[place], sems.at[i + 1, j])
            copy.start()
            copies.append(copy)
    chosen.wait()
    for i, first in enumerate(firsts):
        copies[2 * i].wait()
        copies[2 * i + 1].wait()
        for t in range(HALF):
            place = i * HALF + t
            value = g_ref[place] + r_ref[place]
            value = jnp.where(bitmap[0, first + t] > 0, value, jnp.zeros_like(value))
            outs[place // (2 * BLOCK)][place % (2 * BLOCK)] = value


def outgoing(side, bitmap, gradients, residual):
    vmem = pl.BlockSpec(memory_space=pltpu.VMEM)
    return pl.pallas_call(
        functools.partial(outgoing_kernel, side),
        in_specs=[pl.BlockSpec(memory_space=pl.ANY)] * 3,
        out_specs=[vmem] * 2,
        out_shape=[tiles_shape(2 * BLOCK)] * 2,
        scratch_shapes=[
            pltpu.SMEM((1, 128), jnp.int32),
            pltpu.VMEM((4 * BLOCK, 128, 128), BF16),
            pltpu.VMEM((4 * BLOCK, 128, 128), BF16),
            pltpu.SemaphoreType.DMA((9, 2)),
        ],
        compiler_params=params(),
        cost_estimate=cost(12 * BLOCK),
    )(bitmap, gradients, residual)


def left_kernel(after_ref, bitmap_ref, g_ref, r_ref, out_ref, token_ref):
    first = pl.program_id(0) * BLOCK
    for t in range(BLOCK):
        value = g_ref[t] + r_ref[t]
        out_ref[t] = jnp.where(bitmap_ref[0, first + t] > 0, jnp.zeros_like(value), value)
    token_ref[...] = jnp.zeros_like(token_ref)


def left_over(after, bitmap, gradients, residual):
    block = spec_of(BLOCK, lambda i: (i, 0, 0))
    return pl.pallas_call(
        left_kernel,
        grid=(8,),
        in_specs=[
            pl.BlockSpec(memory_space=pl.ANY),
            pl.BlockSpec(memory_space=pltpu.SMEM),
            block,
            block,
        ],
        out_specs=[block, pl.BlockSpec((8, 128), lambda i: (0, 0))],
        out_shape=[tiles_shape(128), jax.ShapeDtypeStruct((8, 128), F32)],
        compiler_params=params(),
        cost_estimate=cost(3 * 128),
    )(after, bitmap, gradients, residual)


def pair_kernel(a_ref, b_ref, *out_refs):
    for k, out_ref in enumerate(out_refs):

        @pl.when(pl.program_id(0) == k)
        def _():
            out_ref[...] = a_ref[...] + b_ref[...]


def pair_sums(a, b):
    count = a.shape[0] // BLOCK
    return pl.pallas_call(
        pair_kernel,
        grid=(count,),
        in_specs=[spec_of(BLOCK, lambda i: (i, 0, 0))] * 2,
        out_specs=[spec_of(BLOCK, lambda i: (0, 0, 0))] * count,
        out_shape=[tiles_shape(BLOCK)] * count,
        compiler_params=params(),
        cost_estimate=cost(3 * count * BLOCK),
    )(a, b)


def total_kernel(after_ref, r0, r1, r2, r3, low_ref, high_ref):
    for t in range(BLOCK):
        total = (r0[t].astype(F32) + r2[t].astype(F32)) + (r1[t].astype(F32) + r3[t].astype(F32))
        out_ref = low_ref if t < HALF else high_ref
        out_ref[t % HALF] = total.astype(BF16)


def block_total(after, *blocks):
    return pl.pallas_call(
        total_kernel,
        in_specs=[pl.BlockSpec(memory_space=pl.ANY)] + [spec_of(BLOCK, lambda: (0, 0, 0))] * 4,
        out_specs=[spec_of(HALF, lambda: (0, 0, 0))] * 2,
        out_shape=[tiles_shape(HALF)] * 2,
        compiler_params=params(),
        cost_estimate=cost(5 * BLOCK),
    )(after, *blocks)


def halves_kernel(a0, a1, b0, b1, low_ref, high_ref):
    for t in range(HALF):
        low_ref[t] = a0[t] + a1[t]
        high_ref[t] = b0[t] + b1[t]


def halves_sum(*halves):
    return pl.pallas_call(
        halves_kernel,
        in_specs=[spec_of(HALF, lambda: (0, 0, 0))] * 4,
        out_specs=[spec_of(HALF, lambda: (0, 0, 0))] * 2,
        out_shape=[tiles_shape(HALF)] * 2,
        compiler_params=params(),
        cost_estimate=cost(6 * HALF),
    )(*halves)


def put_tile(ref, t, value):
    ref[pl.ds(t * 128, 128), :] = value


def last_kernel(lo_ref, hi_ref, a0, a1, b0, b1, plain_ref, full_ref, row_ref):
    shard = lax.axis_index("tensor")
    lo, hi = lo_ref[pl.ds(shard, 1), :], hi_ref[pl.ds(shard, 1), :]
    first = block_of(0, 0) * BLOCK
    row = jnp.zeros((1, 128), F32)
    for t in range(BLOCK):
        left, right = (a0, a1) if t < HALF else (b0, b1)
        total = left[t % HALF].astype(F32) + right[t % HALF].astype(F32)
        put_tile(plain_ref, t, total.astype(BF16))
        put_tile(full_ref, t, total.astype(BF16))
        square = jnp.sum(jnp.sum(total * total, axis=0, keepdims=True), axis=1, keepdims=True)
        row = row + jnp.where((lo <= first + t) & (first + t < hi), square, 0.0)
    row_ref[...] = jnp.broadcast_to(row, (8, 128))


def flat_shape(tiles, rows):
    return jax.ShapeDtypeStruct((tiles * 128 + rows, 128), BF16)


def last_sum(lo, hi, *halves):
    return pl.pallas_call(
        last_kernel,
        out_shape=[
            flat_shape(BLOCK, 0),
            flat_shape(BLOCK, ROWS),
            jax.ShapeDtypeStruct((8, 128), F32),
        ],
        compiler_params=params(),
        cost_estimate=cost(6 * HALF),
    )(lo, hi, *halves)


def pack_kernel(full_ref, mine_ref, other_ref, out_ref, row_ref, sem):
    row = 0.5 * (mine_ref[0:1, :] + other_ref[0:1, :])
    rest, rows = jnp.broadcast_to(row, (ROWS, 128)), jnp.zeros((ROWS, 128), F32)
    place = lax.broadcasted_iota(jnp.int32, (ROWS, 128), 0)
    for i in range(3):
        part = rest.astype(BF16).astype(F32)
        rows = jnp.where(place == i, part, rows)
        rest = jnp.where(jnp.abs(part) < jnp.inf, rest - part, 0.0)
    row_ref[...] = rows.astype(BF16)
    copy = pltpu.make_async_copy(row_ref, out_ref.at[pl.ds(BLOCK * 128, ROWS), :], sem)
    copy.start()
    copy.wait()


def pack(full, mine, other):
    vmem = pl.BlockSpec(memory_space=pltpu.VMEM)
    anywhere = pl.BlockSpec(memory_space=pl.ANY)
    return pl.pallas_call(
        pack_kernel,
        in_specs=[anywhere, vmem, vmem],
        out_specs=[anywhere, vmem],
        out_shape=[flat_shape(BLOCK, ROWS), flat_shape(0, ROWS)],
        scratch_shapes=[pltpu.SemaphoreType.DMA],
        input_output_aliases={0: 0},
        compiler_params=params(),
        cost_estimate=cost(1),
    )(full, mine, other)


def rows_kernel(r0, r2, r1, r3, out_ref):
    rows = []
    for ref in (r0, r2, r1, r3):
        parts = ref[pl.ds(ref.shape[0] - ROWS, ROWS), :].astype(F32)
        rows.append((parts[0:1, :] + parts[1:2, :]) + parts[2:3, :])
    total = 2.0 * ((rows[0] + rows[1]) + (rows[2] + rows[3]))
    out_ref[...] = jnp.broadcast_to(total, (8, 128))


def sum_of_rows(*smalls):
    return pl.pallas_call(
        rows_kernel,
        out_shape=jax.ShapeDtypeStruct((8, 128), F32),
        compiler_params=params(),
        cost_estimate=cost(1),
    )(*smalls)


def final_kernel(lo_ref, hi_ref, mine_ref, other_ref, m_ref, *refs):
    blocks, (out_ref, factor_ref, ready_ref, sems) = refs[:8], refs[9:]
    shard = lax.axis_index("tensor")
    lo, hi = lo_ref[pl.ds(shard, 1), :], hi_ref[pl.ds(shard, 1), :]
    count = jnp.sum((hi_ref[...] - lo_ref[...]).astype(F32), axis=0, keepdims=True)
    squares = mine_ref[0:1, :] + other_ref[0:1, :]
    rms = jnp.sqrt(squares / (jnp.maximum(count, 1.0) * 16384.0) + EPSILON)
    clip = jnp.minimum(1.0, CLIP_LEVEL / rms)
    tile = lax.broadcasted_iota(jnp.int32, (128, 128), 0)
    chosen = jnp.where((lo <= tile) & (tile < hi), clip, 0.0)
    factor_ref[...] = jnp.broadcast_to(jnp.sum(chosen, axis=1, keepdims=True), (128, 128))

    def tiles_of(source, count, first, place):
        def one_tile(t, carry):
            value = source[pl.ds(pl.multiple_of(t * 128, 128), 128), :]
            update = value.astype(F32) * factor_ref[pl.ds(first + t, 1), :]
            new = MOMENTUM * m_ref[first + t].astype(F32) + update
            ready_ref[place + t] = new.astype(BF16)
            return carry

        lax.fori_loop(0, count, one_tile, 0, unroll=4)

    copies = []
    for k in range(8):
        first = block_of(k % 2, -RETURNED[k // 2]) * BLOCK
        tiles_of(blocks[k], BLOCK, first, k * BLOCK)
        copies.append(
            pltpu.make_async_copy(
                ready_ref.at[pl.ds(k * BLOCK, BLOCK)],
                out_ref.at[pl.ds(first, BLOCK)],
                sems.at[k],
            )
        )
        copies[-1].start()
    for copy in copies:
        copy.wait()


def finish(lo, hi, mine, other, momentum, blocks):
    whole = pl.BlockSpec(memory_space=pltpu.VMEM)
    return pl.pallas_call(
        final_kernel,
        in_specs=[whole] * (5 + len(blocks)),
        out_specs=pl.BlockSpec(memory_space=pl.ANY),
        scratch_shapes=[
            pltpu.VMEM((128, 128), F32),
            pltpu.VMEM((128, 128, 128), BF16),
            pltpu.SemaphoreType.DMA((8,)),
        ],
        out_shape=tiles_shape(128),
        compiler_params=params(20),
        cost_estimate=cost(3 * 128),
    )(lo, hi, mine, other, momentum, *blocks)


def shards(gradients, residual, momentum, bitmap, starts):
    gradients, residual = gradients[0], residual[0]
    lo = jnp.pad(starts, ((0, 0), (0, 96)), constant_values=128)
    hi = jnp.pad(starts[:, 1:], ((0, 0), (0, 97)), constant_values=128)

    gradients = pltpu.with_memory_space_constraint(gradients, pltpu.HBM)
    residual = pltpu.with_memory_space_constraint(residual, pltpu.HBM)
    bitmap = pltpu.with_memory_space_constraint(bitmap, pltpu.HBM)
    arrays = (bitmap, gradients, residual)
    swapped = [send(part, swap_core()) for part in outgoing(1, *arrays)]
    kept = outgoing(0, *arrays)
    one, three = pair_sums(kept[0], swapped[0])
    by_one = send(one, shift_first(1))
    by_three = send(three, shift_first(3))
    two, own = pair_sums(kept[1], swapped[1])
    by_two = send(two, shift_first(2))
    left, token = left_over(two, *arrays)

    low, high = block_total(token, own, by_one, by_two, by_three)
    low, high = halves_sum(low, send(low, swap_second(1)), high, send(high, swap_second(3)))
    plain, full, row = last_sum(
        lo, hi, low, send(low, swap_second(3)), high, send(high, swap_second(1))
    )

    by_two = send(plain, shift_first(2))
    row = row + send(row, swap_tensor(1), "tensor")
    full, row = pack(full, row, send(row, swap_tensor(3), "tensor"))
    by_one, by_three = send(full, shift_first(1)), send(full, shift_first(3))
    row_two = send(row, shift_first(2))
    row = sum_of_rows(full, row_two, by_one, by_three)
    other = send(row, swap_core())
    blocks = [full, send(full, swap_core())]
    for block in (after(by_one, row_two), by_three):
        blocks += [block, send(block, swap_core())]
    token = by_two[:ROWS]
    for _ in range(CHAIN):
        token = send(token, swap_core())
    moved, token = lax.optimization_barrier((by_two, token))
    blocks += [by_two, send(moved, swap_core()), token]
    return (left[None], finish(lo, hi, row, other, momentum, blocks))


def solution(mesh):
    return jax.shard_map(
        shards,
        mesh=mesh,
        in_specs=(
            P("dp", "tensor", None, None),
            P("dp", "tensor", None, None),
            P("tensor", None, None),
            P("dp", "tensor"),
            P(),
        ),
        out_specs=(P("dp", "tensor", None, None), P("tensor", None, None)),
        check_vma=False,
    )
```

```python
import functools

import jax
import jax.numpy as jnp
from jax import lax
from jax.experimental import pallas as pl
from jax.experimental.pallas import tpu as pltpu
from jax.sharding import PartitionSpec as P

MOMENTUM = 0.9
CLIP_LEVEL = 3.0
EPSILON = 1e-06
BF16 = jnp.bfloat16
F32 = jnp.float32
HALF = 8
BLOCK = 16
ROWS = 16
CHAIN = 3
GROUPS = ((1, 3), (2, 0))
RETURNED = (0, 1, 3, 2)
MIB = 2**20


def dp_index(z, x, core):
    return (z * 4 + x) * 2 + core


def each_dp():
    return [(d, d // 8, (d // 2) % 4, d % 2) for d in range(32)]


def swap_core():
    return [(d, d ^ 1) for d in range(32)]


def along(axis, move):
    pairs = []
    for d, z, x, core in each_dp():
        on_x = (core == 0) == (axis == 0)
        to = dp_index(z, move(x), core) if on_x else dp_index(move(z), x, core)
        pairs.append((d, to))
    return pairs


def shift_first(k):
    return along(0, lambda p: (p + k) % 4)


def swap_second(mask):
    return along(1, lambda p: p ^ mask)


def swap_tensor(mask):
    return [(i, i ^ mask) for i in range(4)]


def after(array, earlier):
    return lax.optimization_barrier((array, earlier))[0]


def send(array, pairs, axis="dp"):
    return lax.ppermute(array, axis, pairs)


def places():
    dp = lax.axis_index("dp")
    z, x, core = lax.div(dp, 8), lax.rem(lax.div(dp, 2), 4), lax.rem(dp, 2)
    return core, jnp.where(core == 0, x, z), jnp.where(core == 0, z, x)


def block_of(side, shift):
    core, mine, theirs = places()
    if side:
        core, mine = 1 - core, theirs
    return core * 4 + lax.rem(mine + shift + 4, 4)


def spec_of(tiles, index_map):
    return pl.BlockSpec((tiles, 128, 128), index_map)


def tiles_shape(count):
    return jax.ShapeDtypeStruct((count, 128, 128), BF16)


def params(mib=40):
    return pltpu.CompilerParams(vmem_limit_bytes=mib * MIB)


def cost(tiles_read_or_written):
    return pl.CostEstimate(
        flops=tiles_read_or_written * 16384,
        bytes_accessed=tiles_read_or_written * 32768,
        transcendentals=0,
    )


def outgoing_kernel(side, bitmap_hbm, g_hbm, r_hbm, *refs):
    outs, (bitmap, g_ref, r_ref, sems) = refs[:2], refs[2:]
    shifts = [k for group in GROUPS for k in group]
    firsts = [block_of(side, k) * BLOCK + h * HALF for k in shifts for h in range(2)]
    chosen = pltpu.make_async_copy(bitmap_hbm, bitmap, sems.at[0, 0])
    chosen.start()
    copies = []
    for i, first in enumerate(firsts):
        rows, place = pl.ds(first, HALF), pl.ds(i * HALF, HALF)
        for j, (source, target) in enumerate(((g_hbm, g_ref), (r_hbm, r_ref))):
            copy = pltpu.make_async_copy(source.at[rows], target.at[place], sems.at[i + 1, j])
            copy.start()
            copies.append(copy)
    chosen.wait()
    for i, first in enumerate(firsts):
        copies[2 * i].wait()
        copies[2 * i + 1].wait()
        for t in range(HALF):
            place = i * HALF + t
            value = g_ref[place] + r_ref[place]
            value = jnp.where(bitmap[0, first + t] > 0, value, jnp.zeros_like(value))
            outs[place // (2 * BLOCK)][place % (2 * BLOCK)] = value


def outgoing(side, bitmap, gradients, residual):
    vmem = pl.BlockSpec(memory_space=pltpu.VMEM)
    return pl.pallas_call(
        functools.partial(outgoing_kernel, side),
        in_specs=[pl.BlockSpec(memory_space=pl.ANY)] * 3,
        out_specs=[vmem] * 2,
        out_shape=[tiles_shape(2 * BLOCK)] * 2,
        scratch_shapes=[
            pltpu.SMEM((1, 128), jnp.int32),
            pltpu.VMEM((4 * BLOCK, 128, 128), BF16),
            pltpu.VMEM((4 * BLOCK, 128, 128), BF16),
            pltpu.SemaphoreType.DMA((9, 2)),
        ],
        compiler_params=params(),
        cost_estimate=cost(12 * BLOCK),
    )(bitmap, gradients, residual)


def left_kernel(after_ref, bitmap_ref, g_ref, r_ref, out_ref, token_ref):
    first = pl.program_id(0) * BLOCK
    for t in range(BLOCK):
        value = g_ref[t] + r_ref[t]
        out_ref[t] = jnp.where(bitmap_ref[0, first + t] > 0, jnp.zeros_like(value), value)
    token_ref[...] = jnp.zeros_like(token_ref)


def left_over(after, bitmap, gradients, residual):
    block = spec_of(BLOCK, lambda i: (i, 0, 0))
    return pl.pallas_call(
        left_kernel,
        grid=(8,),
        in_specs=[
            pl.BlockSpec(memory_space=pl.ANY),
            pl.BlockSpec(memory_space=pltpu.SMEM),
            block,
            block,
        ],
        out_specs=[block, pl.BlockSpec((8, 128), lambda i: (0, 0))],
        out_shape=[tiles_shape(128), jax.ShapeDtypeStruct((8, 128), F32)],
        compiler_params=params(),
        cost_estimate=cost(3 * 128),
    )(after, bitmap, gradients, residual)


def pair_kernel(a_ref, b_ref, *out_refs):
    for k, out_ref in enumerate(out_refs):

        @pl.when(pl.program_id(0) == k)
        def _():
            out_ref[...] = a_ref[...] + b_ref[...]


def pair_sums(a, b):
    count = a.shape[0] // BLOCK
    return pl.pallas_call(
        pair_kernel,
        grid=(count,),
        in_specs=[spec_of(BLOCK, lambda i: (i, 0, 0))] * 2,
        out_specs=[spec_of(BLOCK, lambda i: (0, 0, 0))] * count,
        out_shape=[tiles_shape(BLOCK)] * count,
        compiler_params=params(),
        cost_estimate=cost(3 * count * BLOCK),
    )(a, b)


def total_kernel(after_ref, r0, r1, r2, r3, low_ref, high_ref):
    for t in range(BLOCK):
        total = (r0[t].astype(F32) + r2[t].astype(F32)) + (r1[t].astype(F32) + r3[t].astype(F32))
        out_ref = low_ref if t < HALF else high_ref
        out_ref[t % HALF] = total.astype(BF16)


def block_total(after, *blocks):
    return pl.pallas_call(
        total_kernel,
        in_specs=[pl.BlockSpec(memory_space=pl.ANY)] + [spec_of(BLOCK, lambda: (0, 0, 0))] * 4,
        out_specs=[spec_of(HALF, lambda: (0, 0, 0))] * 2,
        out_shape=[tiles_shape(HALF)] * 2,
        compiler_params=params(),
        cost_estimate=cost(5 * BLOCK),
    )(after, *blocks)


def halves_kernel(a0, a1, b0, b1, low_ref, high_ref):
    for t in range(HALF):
        low_ref[t] = a0[t] + a1[t]
        high_ref[t] = b0[t] + b1[t]


def halves_sum(*halves):
    return pl.pallas_call(
        halves_kernel,
        in_specs=[spec_of(HALF, lambda: (0, 0, 0))] * 4,
        out_specs=[spec_of(HALF, lambda: (0, 0, 0))] * 2,
        out_shape=[tiles_shape(HALF)] * 2,
        compiler_params=params(),
        cost_estimate=cost(6 * HALF),
    )(*halves)


def put_tile(ref, t, value):
    ref[pl.ds(t * 128, 128), :] = value


def last_kernel(lo_ref, hi_ref, a0, a1, b0, b1, plain_ref, full_ref, row_ref):
    shard = lax.axis_index("tensor")
    lo, hi = lo_ref[pl.ds(shard, 1), :], hi_ref[pl.ds(shard, 1), :]
    first = block_of(0, 0) * BLOCK
    row = jnp.zeros((1, 128), F32)
    for t in range(BLOCK):
        left, right = (a0, a1) if t < HALF else (b0, b1)
        total = left[t % HALF].astype(F32) + right[t % HALF].astype(F32)
        put_tile(plain_ref, t, total.astype(BF16))
        put_tile(full_ref, t, total.astype(BF16))
        square = jnp.sum(jnp.sum(total * total, axis=0, keepdims=True), axis=1, keepdims=True)
        row = row + jnp.where((lo <= first + t) & (first + t < hi), square, 0.0)
    row_ref[...] = jnp.broadcast_to(row, (8, 128))


def flat_shape(tiles, rows):
    return jax.ShapeDtypeStruct((tiles * 128 + rows, 128), BF16)


def last_sum(lo, hi, *halves):
    return pl.pallas_call(
        last_kernel,
        out_shape=[
            flat_shape(BLOCK, 0),
            flat_shape(BLOCK, ROWS),
            jax.ShapeDtypeStruct((8, 128), F32),
        ],
        compiler_params=params(),
        cost_estimate=cost(6 * HALF),
    )(lo, hi, *halves)


def pack_kernel(full_ref, mine_ref, other_ref, out_ref, row_ref, sem):
    row = 0.5 * (mine_ref[0:1, :] + other_ref[0:1, :])
    rest, rows = jnp.broadcast_to(row, (ROWS, 128)), jnp.zeros((ROWS, 128), F32)
    place = lax.broadcasted_iota(jnp.int32, (ROWS, 128), 0)
    for i in range(3):
        part = rest.astype(BF16).astype(F32)
        rows = jnp.where(place == i, part, rows)
        rest = jnp.where(jnp.abs(part) < jnp.inf, rest - part, 0.0)
    row_ref[...] = rows.astype(BF16)
    copy = pltpu.make_async_copy(row_ref, out_ref.at[pl.ds(BLOCK * 128, ROWS), :], sem)
    copy.start()
    copy.wait()


def pack(full, mine, other):
    vmem = pl.BlockSpec(memory_space=pltpu.VMEM)
    anywhere = pl.BlockSpec(memory_space=pl.ANY)
    return pl.pallas_call(
        pack_kernel,
        in_specs=[anywhere, vmem, vmem],
        out_specs=[anywhere, vmem],
        out_shape=[flat_shape(BLOCK, ROWS), flat_shape(0, ROWS)],
        scratch_shapes=[pltpu.SemaphoreType.DMA],
        input_output_aliases={0: 0},
        compiler_params=params(),
        cost_estimate=cost(1),
    )(full, mine, other)


def rows_kernel(r0, r2, r1, r3, out_ref):
    rows = []
    for ref in (r0, r2, r1, r3):
        parts = ref[pl.ds(ref.shape[0] - ROWS, ROWS), :].astype(F32)
        rows.append((parts[0:1, :] + parts[1:2, :]) + parts[2:3, :])
    total = 2.0 * ((rows[0] + rows[1]) + (rows[2] + rows[3]))
    out_ref[...] = jnp.broadcast_to(total, (8, 128))


def sum_of_rows(*smalls):
    return pl.pallas_call(
        rows_kernel,
        out_shape=jax.ShapeDtypeStruct((8, 128), F32),
        compiler_params=params(),
        cost_estimate=cost(1),
    )(*smalls)


def final_kernel(lo_ref, hi_ref, mine_ref, other_ref, m_ref, *refs):
    blocks, (out_ref, factor_ref, ready_ref, sems) = refs[:8], refs[9:]
    shard = lax.axis_index("tensor")
    lo, hi = lo_ref[pl.ds(shard, 1), :], hi_ref[pl.ds(shard, 1), :]
    count = jnp.sum((hi_ref[...] - lo_ref[...]).astype(F32), axis=0, keepdims=True)
    squares = mine_ref[0:1, :] + other_ref[0:1, :]
    rms = jnp.sqrt(squares / (jnp.maximum(count, 1.0) * 16384.0) + EPSILON)
    clip = jnp.minimum(1.0, CLIP_LEVEL / rms)
    tile = lax.broadcasted_iota(jnp.int32, (128, 128), 0)
    chosen = jnp.where((lo <= tile) & (tile < hi), clip, 0.0)
    factor_ref[...] = jnp.broadcast_to(jnp.sum(chosen, axis=1, keepdims=True), (128, 128))

    def tiles_of(source, start, first, place):
        def one_tile(t, carry):
            value = source[pl.ds(pl.multiple_of(t * 128, 128), 128), :]
            update = value.astype(F32) * factor_ref[pl.ds(first + t, 1), :]
            new = MOMENTUM * m_ref[first + t].astype(F32) + update
            ready_ref[place + t] = new.astype(BF16)
            return carry

        lax.fori_loop(start, start + HALF, one_tile, 0, unroll=HALF)

    copies = []
    for k in range(8):
        first = block_of(k % 2, -RETURNED[k // 2]) * BLOCK
        for half in range(2):
            start, place = half * HALF, k * BLOCK + half * HALF
            tiles_of(blocks[k], start, first, k * BLOCK)
            copies.append(
                pltpu.make_async_copy(
                    ready_ref.at[pl.ds(place, HALF)],
                    out_ref.at[pl.ds(first + start, HALF)],
                    sems.at[2 * k + half],
                )
            )
            copies[-1].start()
    for copy in copies:
        copy.wait()


def finish(lo, hi, mine, other, momentum, blocks):
    whole = pl.BlockSpec(memory_space=pltpu.VMEM)
    return pl.pallas_call(
        final_kernel,
        in_specs=[whole] * (5 + len(blocks)),
        out_specs=pl.BlockSpec(memory_space=pl.ANY),
        scratch_shapes=[
            pltpu.VMEM((128, 128), F32),
            pltpu.VMEM((128, 128, 128), BF16),
            pltpu.SemaphoreType.DMA((16,)),
        ],
        out_shape=tiles_shape(128),
        compiler_params=params(20),
        cost_estimate=cost(3 * 128),
    )(lo, hi, mine, other, momentum, *blocks)


def shards(gradients, residual, momentum, bitmap, starts):
    gradients, residual = gradients[0], residual[0]
    lo = jnp.pad(starts, ((0, 0), (0, 96)), constant_values=128)
    hi = jnp.pad(starts[:, 1:], ((0, 0), (0, 97)), constant_values=128)

    gradients = pltpu.with_memory_space_constraint(gradients, pltpu.HBM)
    residual = pltpu.with_memory_space_constraint(residual, pltpu.HBM)
    bitmap = pltpu.with_memory_space_constraint(bitmap, pltpu.HBM)
    arrays = (bitmap, gradients, residual)
    swapped = [send(part, swap_core()) for part in outgoing(1, *arrays)]
    kept = outgoing(0, *arrays)
    one, three = pair_sums(kept[0], swapped[0])
    by_one = send(one, shift_first(1))
    by_three = send(three, shift_first(3))
    two, own = pair_sums(kept[1], swapped[1])
    by_two = send(two, shift_first(2))
    left, token = left_over(two, *arrays)

    low, high = block_total(token, own, by_one, by_two, by_three)
    low, high = halves_sum(low, send(low, swap_second(1)), high, send(high, swap_second(3)))
    plain, full, row = last_sum(
        lo, hi, low, send(low, swap_second(3)), high, send(high, swap_second(1))
    )

    by_two = send(plain, shift_first(2))
    row = row + send(row, swap_tensor(1), "tensor")
    full, row = pack(full, row, send(row, swap_tensor(3), "tensor"))
    by_one, by_three = send(full, shift_first(1)), send(full, shift_first(3))
    row_two = send(row, shift_first(2))
    row = sum_of_rows(full, row_two, by_one, by_three)
    other = send(row, swap_core())
    blocks = [full, send(full, swap_core())]
    for block in (after(by_one, row_two), by_three):
        blocks += [block, send(block, swap_core())]
    token = by_two[:ROWS]
    for _ in range(CHAIN):
        token = send(token, swap_core())
    moved, token = lax.optimization_barrier((by_two, token))
    blocks += [by_two, send(moved, swap_core()), token]
    return (left[None], finish(lo, hi, row, other, momentum, blocks))


def solution(mesh):
    return jax.shard_map(
        shards,
        mesh=mesh,
        in_specs=(
            P("dp", "tensor", None, None),
            P("dp", "tensor", None, None),
            P("tensor", None, None),
            P("dp", "tensor"),
            P(),
        ),
        out_specs=(P("dp", "tensor", None, None), P("tensor", None, None)),
        check_vma=False,
    )
```

```python
import functools

import jax
import jax.numpy as jnp
from jax import lax
from jax.experimental import pallas as pl
from jax.experimental.pallas import tpu as pltpu
from jax.sharding import PartitionSpec as P

MOMENTUM = 0.9
CLIP_LEVEL = 3.0
EPSILON = 1e-06
BF16 = jnp.bfloat16
F32 = jnp.float32
HALF = 8
BLOCK = 16
ROWS = 16
GROUPS = ((1, 3), (2, 0))
RETURNED = (0, 1, 3, 2)
MIB = 2**20


def dp_index(z, x, core):
    return (z * 4 + x) * 2 + core


def each_dp():
    return [(d, d // 8, (d // 2) % 4, d % 2) for d in range(32)]


def swap_core():
    return [(d, d ^ 1) for d in range(32)]


def along(axis, move):
    pairs = []
    for d, z, x, core in each_dp():
        on_x = (core == 0) == (axis == 0)
        to = dp_index(z, move(x), core) if on_x else dp_index(move(z), x, core)
        pairs.append((d, to))
    return pairs


def shift_first(k):
    return along(0, lambda p: (p + k) % 4)


def swap_second(mask):
    return along(1, lambda p: p ^ mask)


def swap_tensor(mask):
    return [(i, i ^ mask) for i in range(4)]


def after(array, earlier):
    return lax.optimization_barrier((array, earlier))[0]


def send(array, pairs, axis="dp"):
    return lax.ppermute(array, axis, pairs)


def places():
    dp = lax.axis_index("dp")
    z, x, core = lax.div(dp, 8), lax.rem(lax.div(dp, 2), 4), lax.rem(dp, 2)
    return core, jnp.where(core == 0, x, z), jnp.where(core == 0, z, x)


def block_of(side, shift):
    core, mine, theirs = places()
    if side:
        core, mine = 1 - core, theirs
    return core * 4 + lax.rem(mine + shift + 4, 4)


def spec_of(tiles, index_map):
    return pl.BlockSpec((tiles, 128, 128), index_map)


def tiles_shape(count):
    return jax.ShapeDtypeStruct((count, 128, 128), BF16)


def params(mib=40):
    return pltpu.CompilerParams(vmem_limit_bytes=mib * MIB)


def cost(tiles_read_or_written):
    return pl.CostEstimate(
        flops=tiles_read_or_written * 16384,
        bytes_accessed=tiles_read_or_written * 32768,
        transcendentals=0,
    )


def outgoing_kernel(side, bitmap_hbm, g_hbm, r_hbm, *refs):
    outs, (bitmap, g_ref, r_ref, sems) = refs[:2], refs[2:]
    shifts = [k for group in GROUPS for k in group]
    firsts = [block_of(side, k) * BLOCK + h * HALF for k in shifts for h in range(2)]
    chosen = pltpu.make_async_copy(bitmap_hbm, bitmap, sems.at[0, 0])
    chosen.start()
    copies = []
    for i, first in enumerate(firsts):
        rows, place = pl.ds(first, HALF), pl.ds(i * HALF, HALF)
        for j, (source, target) in enumerate(((g_hbm, g_ref), (r_hbm, r_ref))):
            copy = pltpu.make_async_copy(source.at[rows], target.at[place], sems.at[i + 1, j])
            copy.start()
            copies.append(copy)
    chosen.wait()
    for i, first in enumerate(firsts):
        copies[2 * i].wait()
        copies[2 * i + 1].wait()
        for t in range(HALF):
            place = i * HALF + t
            value = g_ref[place] + r_ref[place]
            value = jnp.where(bitmap[0, first + t] > 0, value, jnp.zeros_like(value))
            outs[place // (2 * BLOCK)][place % (2 * BLOCK)] = value


def outgoing(side, bitmap, gradients, residual):
    vmem = pl.BlockSpec(memory_space=pltpu.VMEM)
    return pl.pallas_call(
        functools.partial(outgoing_kernel, side),
        in_specs=[pl.BlockSpec(memory_space=pl.ANY)] * 3,
        out_specs=[vmem] * 2,
        out_shape=[tiles_shape(2 * BLOCK)] * 2,
        scratch_shapes=[
            pltpu.SMEM((1, 128), jnp.int32),
            pltpu.VMEM((4 * BLOCK, 128, 128), BF16),
            pltpu.VMEM((4 * BLOCK, 128, 128), BF16),
            pltpu.SemaphoreType.DMA((9, 2)),
        ],
        compiler_params=params(),
        cost_estimate=cost(12 * BLOCK),
    )(bitmap, gradients, residual)


def left_kernel(after_ref, bitmap_ref, g_ref, r_ref, out_ref, token_ref):
    first = pl.program_id(0) * BLOCK
    for t in range(BLOCK):
        value = g_ref[t] + r_ref[t]
        out_ref[t] = jnp.where(bitmap_ref[0, first + t] > 0, jnp.zeros_like(value), value)
    token_ref[...] = jnp.zeros_like(token_ref)


def left_over(after, bitmap, gradients, residual):
    block = spec_of(BLOCK, lambda i: (i, 0, 0))
    return pl.pallas_call(
        left_kernel,
        grid=(8,),
        in_specs=[
            pl.BlockSpec(memory_space=pl.ANY),
            pl.BlockSpec(memory_space=pltpu.SMEM),
            block,
            block,
        ],
        out_specs=[block, pl.BlockSpec((8, 128), lambda i: (0, 0))],
        out_shape=[tiles_shape(128), jax.ShapeDtypeStruct((8, 128), F32)],
        compiler_params=params(),
        cost_estimate=cost(3 * 128),
    )(after, bitmap, gradients, residual)


def pair_kernel(a_ref, b_ref, *out_refs):
    for k, out_ref in enumerate(out_refs):

        @pl.when(pl.program_id(0) == k)
        def _():
            out_ref[...] = a_ref[...] + b_ref[...]


def pair_sums(a, b):
    count = a.shape[0] // BLOCK
    return pl.pallas_call(
        pair_kernel,
        grid=(count,),
        in_specs=[spec_of(BLOCK, lambda i: (i, 0, 0))] * 2,
        out_specs=[spec_of(BLOCK, lambda i: (0, 0, 0))] * count,
        out_shape=[tiles_shape(BLOCK)] * count,
        compiler_params=params(),
        cost_estimate=cost(3 * count * BLOCK),
    )(a, b)


def total_kernel(after_ref, r0, r1, r2, r3, low_ref, high_ref):
    for t in range(BLOCK):
        total = (r0[t].astype(F32) + r2[t].astype(F32)) + (r1[t].astype(F32) + r3[t].astype(F32))
        out_ref = low_ref if t < HALF else high_ref
        out_ref[t % HALF] = total.astype(BF16)


def block_total(after, *blocks):
    return pl.pallas_call(
        total_kernel,
        in_specs=[pl.BlockSpec(memory_space=pl.ANY)] + [spec_of(BLOCK, lambda: (0, 0, 0))] * 4,
        out_specs=[spec_of(HALF, lambda: (0, 0, 0))] * 2,
        out_shape=[tiles_shape(HALF)] * 2,
        compiler_params=params(),
        cost_estimate=cost(5 * BLOCK),
    )(after, *blocks)


def halves_kernel(a0, a1, b0, b1, low_ref, high_ref):
    for t in range(HALF):
        low_ref[t] = a0[t] + a1[t]
        high_ref[t] = b0[t] + b1[t]


def halves_sum(*halves):
    return pl.pallas_call(
        halves_kernel,
        in_specs=[spec_of(HALF, lambda: (0, 0, 0))] * 4,
        out_specs=[spec_of(HALF, lambda: (0, 0, 0))] * 2,
        out_shape=[tiles_shape(HALF)] * 2,
        compiler_params=params(),
        cost_estimate=cost(6 * HALF),
    )(*halves)


def put_tile(ref, t, value):
    ref[pl.ds(t * 128, 128), :] = value


def last_kernel(lo_ref, hi_ref, a0, a1, b0, b1, plain_ref, full_ref, row_ref):
    shard = lax.axis_index("tensor")
    lo, hi = lo_ref[pl.ds(shard, 1), :], hi_ref[pl.ds(shard, 1), :]
    first = block_of(0, 0) * BLOCK
    row = jnp.zeros((1, 128), F32)
    for t in range(BLOCK):
        left, right = (a0, a1) if t < HALF else (b0, b1)
        total = left[t % HALF].astype(F32) + right[t % HALF].astype(F32)
        put_tile(plain_ref, t, total.astype(BF16))
        put_tile(full_ref, t, total.astype(BF16))
        square = jnp.sum(jnp.sum(total * total, axis=0, keepdims=True), axis=1, keepdims=True)
        row = row + jnp.where((lo <= first + t) & (first + t < hi), square, 0.0)
    row_ref[...] = jnp.broadcast_to(row, (8, 128))


def flat_shape(tiles, rows):
    return jax.ShapeDtypeStruct((tiles * 128 + rows, 128), BF16)


def last_sum(lo, hi, *halves):
    return pl.pallas_call(
        last_kernel,
        out_shape=[
            flat_shape(BLOCK, 0),
            flat_shape(BLOCK, ROWS),
            jax.ShapeDtypeStruct((8, 128), F32),
        ],
        compiler_params=params(),
        cost_estimate=cost(6 * HALF),
    )(lo, hi, *halves)


def pack_kernel(full_ref, mine_ref, other_ref, out_ref, row_ref, sem):
    row = 0.5 * (mine_ref[0:1, :] + other_ref[0:1, :])
    rest, rows = jnp.broadcast_to(row, (ROWS, 128)), jnp.zeros((ROWS, 128), F32)
    place = lax.broadcasted_iota(jnp.int32, (ROWS, 128), 0)
    for i in range(3):
        part = rest.astype(BF16).astype(F32)
        rows = jnp.where(place == i, part, rows)
        rest = jnp.where(jnp.abs(part) < jnp.inf, rest - part, 0.0)
    row_ref[...] = rows.astype(BF16)
    copy = pltpu.make_async_copy(row_ref, out_ref.at[pl.ds(BLOCK * 128, ROWS), :], sem)
    copy.start()
    copy.wait()


def pack(full, mine, other):
    vmem = pl.BlockSpec(memory_space=pltpu.VMEM)
    anywhere = pl.BlockSpec(memory_space=pl.ANY)
    return pl.pallas_call(
        pack_kernel,
        in_specs=[anywhere, vmem, vmem],
        out_specs=[anywhere, vmem],
        out_shape=[flat_shape(BLOCK, ROWS), flat_shape(0, ROWS)],
        scratch_shapes=[pltpu.SemaphoreType.DMA],
        input_output_aliases={0: 0},
        compiler_params=params(),
        cost_estimate=cost(1),
    )(full, mine, other)


def rows_kernel(r0, r2, r1, r3, out_ref):
    rows = []
    for ref in (r0, r2, r1, r3):
        parts = ref[pl.ds(ref.shape[0] - ROWS, ROWS), :].astype(F32)
        rows.append((parts[0:1, :] + parts[1:2, :]) + parts[2:3, :])
    total = 2.0 * ((rows[0] + rows[1]) + (rows[2] + rows[3]))
    out_ref[...] = jnp.broadcast_to(total, (8, 128))


def sum_of_rows(*smalls):
    return pl.pallas_call(
        rows_kernel,
        out_shape=jax.ShapeDtypeStruct((8, 128), F32),
        compiler_params=params(),
        cost_estimate=cost(1),
    )(*smalls)


def final_kernel(lo_ref, hi_ref, mine_ref, other_ref, m_ref, *refs):
    blocks, (out_ref, factor_ref, ready_ref, sems) = refs[:8], refs[9:]
    shard = lax.axis_index("tensor")
    lo, hi = lo_ref[pl.ds(shard, 1), :], hi_ref[pl.ds(shard, 1), :]
    count = jnp.sum((hi_ref[...] - lo_ref[...]).astype(F32), axis=0, keepdims=True)
    squares = mine_ref[0:1, :] + other_ref[0:1, :]
    rms = jnp.sqrt(squares / (jnp.maximum(count, 1.0) * 16384.0) + EPSILON)
    clip = jnp.minimum(1.0, CLIP_LEVEL / rms)
    tile = lax.broadcasted_iota(jnp.int32, (128, 128), 0)
    chosen = jnp.where((lo <= tile) & (tile < hi), clip, 0.0)
    factor_ref[...] = jnp.broadcast_to(jnp.sum(chosen, axis=1, keepdims=True), (128, 128))

    def tiles_of(source, start, first, place):
        def one_tile(t, carry):
            value = source[pl.ds(pl.multiple_of(t * 128, 128), 128), :]
            update = value.astype(F32) * factor_ref[pl.ds(first + t, 1), :]
            new = MOMENTUM * m_ref[first + t].astype(F32) + update
            ready_ref[place + t] = new.astype(BF16)
            return carry

        lax.fori_loop(start, start + HALF, one_tile, 0, unroll=HALF)

    copies = []
    for k in range(8):
        first = block_of(k % 2, -RETURNED[k // 2]) * BLOCK
        for half in range(2):
            start, place = half * HALF, k * BLOCK + half * HALF
            tiles_of(blocks[k], start, first, k * BLOCK)
            copies.append(
                pltpu.make_async_copy(
                    ready_ref.at[pl.ds(place, HALF)],
                    out_ref.at[pl.ds(first + start, HALF)],
                    sems.at[2 * k + half],
                )
            )
            copies[-1].start()
    for copy in copies:
        copy.wait()


def finish(lo, hi, mine, other, momentum, blocks):
    whole = pl.BlockSpec(memory_space=pltpu.VMEM)
    return pl.pallas_call(
        final_kernel,
        in_specs=[whole] * (5 + len(blocks)),
        out_specs=pl.BlockSpec(memory_space=pl.ANY),
        scratch_shapes=[
            pltpu.VMEM((128, 128), F32),
            pltpu.VMEM((128, 128, 128), BF16),
            pltpu.SemaphoreType.DMA((16,)),
        ],
        out_shape=tiles_shape(128),
        compiler_params=params(20),
        cost_estimate=cost(3 * 128),
    )(lo, hi, mine, other, momentum, *blocks)


def shards(gradients, residual, momentum, bitmap, starts):
    gradients, residual = gradients[0], residual[0]
    lo = jnp.pad(starts, ((0, 0), (0, 96)), constant_values=128)
    hi = jnp.pad(starts[:, 1:], ((0, 0), (0, 97)), constant_values=128)

    gradients = pltpu.with_memory_space_constraint(gradients, pltpu.HBM)
    residual = pltpu.with_memory_space_constraint(residual, pltpu.HBM)
    bitmap = pltpu.with_memory_space_constraint(bitmap, pltpu.HBM)
    arrays = (bitmap, gradients, residual)
    swapped = [send(part, swap_core()) for part in outgoing(1, *arrays)]
    kept = outgoing(0, *arrays)
    one, three = pair_sums(kept[0], swapped[0])
    by_one = send(one, shift_first(1))
    by_three = send(three, shift_first(3))
    two, own = pair_sums(kept[1], swapped[1])
    by_two = send(two, shift_first(2))
    left, token = left_over(two, *arrays)

    low, high = block_total(token, own, by_one, by_two, by_three)
    low, high = halves_sum(low, send(low, swap_second(1)), high, send(high, swap_second(3)))
    plain, full, row = last_sum(
        lo, hi, low, send(low, swap_second(3)), high, send(high, swap_second(1))
    )

    by_two = send(plain, shift_first(2))
    row = row + send(row, swap_tensor(1), "tensor")
    full, row = pack(full, row, send(row, swap_tensor(3), "tensor"))
    by_one, by_three = send(full, shift_first(1)), send(full, shift_first(3))
    row_two = send(row, shift_first(2))
    row = sum_of_rows(full, row_two, by_one, by_three)
    other = send(row, swap_core())
    token = by_two[:ROWS]
    for _ in range(2):
        token = send(token, swap_core())
    moved, token = lax.optimization_barrier((by_two, token))
    two = send(moved, swap_core())
    moved, token, row_two = lax.optimization_barrier((by_one, token, row_two))
    blocks = [full, send(full, swap_core()), by_one, send(moved, swap_core())]
    blocks += [by_three, send(by_three, swap_core()), by_two, two, token]
    return (left[None], finish(lo, hi, row, other, momentum, blocks))


def solution(mesh):
    return jax.shard_map(
        shards,
        mesh=mesh,
        in_specs=(
            P("dp", "tensor", None, None),
            P("dp", "tensor", None, None),
            P("tensor", None, None),
            P("dp", "tensor"),
            P(),
        ),
        out_specs=(P("dp", "tensor", None, None), P("tensor", None, None)),
        check_vma=False,
    )
```
